32 devices in a mesh: site: 4 (over y, core), bond: 8 (over z, x).
Axes of the slice: x: 2, y: 2, z: 4, core: 2. Of those that a mesh axis runs over, the one named last changes fastest.
Arguments:
- left_start: float32 [2048, 1024], P('bond'), may hold values from -6 to 6
- site_mats: float32 [4, 2, 2048, 2048], P('site', None, 'bond'), may hold values from -0.125 to 0.125
- clicks: int32 [4, 1024], P('site'), may hold values 0 or 1
Outputs:
- final_states: float32 [2048, 1024], P('bond', 'site')
The draws below stay inside these ranges and needn't reach their ends.
All inputs are finite; a program needn't handle non-finite values. No bound on the sum of `clicks` on one device may be relied on, other than what follows from the above.
Results may differ from the reference program's by a relative error of at most 0.00026.
Values sent between devices are 32-bit elements; how exact they have to be, the bound alone decides.
No kernel may reach another device: no remote copies, remote signals or barrier semaphores. Data moves between devices by JAX's collectives and lax.ppermute only.
A program may use at most 64 MiB of HBM per device.

```python
import jax
import jax.numpy as jnp
from jax import lax

BOND = 2048
SITES = 4
SAMPLES = 1024


def place_ends(drawn, stream_key, least, top_value):
    extent = drawn.shape
    index_at = [jax.random.randint(jax.random.fold_in(stream_key, axis), (), 0, extent[axis]) for axis in range(len(extent))]
    drawn = drawn.at[tuple(index_at)].set(least)
    longest = extent.index(max(extent))
    index_at[longest] = (index_at[longest] + 1) % extent[longest]
    return drawn.at[tuple(index_at)].set(top_value)


def levels(key, dims, shards, smallest, largest):
    def one(axis_at, shards_of):
        heights = jax.random.uniform(jax.random.fold_in(jax.random.fold_in(key, 6), axis_at), (shards_of,), jnp.float32, smallest / len(shards), largest / len(shards))
        return jnp.repeat(jnp.exp(heights), dims[axis_at] // shards_of).reshape((-1,) + (1,) * (len(dims) - axis_at - 1))

    loudness = one(*shards[0])
    for cut in shards[1:]:
        loudness = loudness * one(*cut)
    return loudness


def centred(rng, shape, spread, limit, pieces=(), held_as=jnp.bfloat16):
    drawn = spread * jax.random.normal(rng, shape, jnp.float32)
    if pieces:
        drawn = drawn * levels(rng, shape, pieces, -0.22, 0.18)
    return jnp.clip(drawn, -limit, limit).astype(held_as)


def setup_inputs(seed: int = 0) -> dict:
    arg_keys = jax.random.split(jax.random.key(seed), 4)
    return {
        "left_start": centred(arg_keys[0], (BOND, SAMPLES), 1.0, 6.0, ((0, 8),), jnp.float32),
        "site_mats": centred(arg_keys[1], (SITES, 2, BOND, BOND), BOND ** -0.5, 0.125, ((0, 4), (2, 8)), jnp.float32),
        "clicks": place_ends((jax.random.randint(arg_keys[2], (SITES, SAMPLES), 0, 2) < 1).astype(jnp.int32), jax.random.fold_in(arg_keys[2], 1), 0, 1),
    }


def reference(left_start, site_mats, clicks):
    states = left_start
    for index in range(SITES):
        first = jnp.dot(site_mats[index, 0], states, precision=lax.Precision.HIGHEST, preferred_element_type=jnp.float32)
        second = jnp.dot(site_mats[index, 1], states, precision=lax.Precision.HIGHEST, preferred_element_type=jnp.float32)
        states = jnp.where(clicks[index:index + 1, :] == 1, second, first)
    return states
```

```python
import functools

import jax
import jax.numpy as jnp
from jax import lax
from jax.experimental import pallas as pl
from jax.experimental.pallas import tpu as pltpu
from jax.sharding import PartitionSpec as P


class Grid:
    def __init__(self, sites, bonds):
        self.sites, self.bonds = sites, bonds
        self.cores = 2 if sites % 2 == 0 else 1
        self.ny = sites // self.cores
        self.nx = max(q for q in range(1, bonds + 1) if bonds % q == 0 and q * q <= bonds)
        self.nz = bonds // self.nx

    def here(self):
        site, bond = lax.axis_index("site"), lax.axis_index("bond")
        return bond // self.nx, bond % self.nx, site // self.cores, site % self.cores

    def index(self, z, x, y, core):
        site = (y % self.ny) * self.cores + core % self.cores
        return site * self.bonds + (z % self.nz) * self.nx + x % self.nx

    def send(self, value, dz=0, dx=0, dy=0, dcore=0, cores=None, rows=None):
        pairs = []
        for z in range(self.nz):
            for x in range(self.nx):
                for y in range(self.ny) if rows is None else rows:
                    for core in range(self.cores) if cores is None else cores:
                        pairs.append((self.index(z, x, y, core), self.index(z + dz, x + dx, y + dy, core + dcore)))
        return lax.ppermute(value, ("site", "bond"), pairs)


def halves(value):
    high = value.astype(jnp.bfloat16)
    low = (value - high.astype(jnp.float32)).astype(jnp.bfloat16)
    return high, low


def dot3(a, b):
    dot = functools.partial(jnp.dot, preferred_element_type=jnp.float32)
    return dot(a[0], b[0]) + (dot(a[0], b[1]) + dot(a[1], b[0]))


def pack(grid, mats, rows, strip):
    z, x, y, _ = grid.here()
    outcomes = mats.shape[0]
    width = grid.nz * strip
    parts = []
    for dx in range(grid.nx):
        for dy in range(grid.ny):
            strips = []
            for d in range(grid.nz):
                start = ((z - d) % grid.nz) * grid.nx * rows + ((x + dx) % grid.nx) * rows + ((y + dy) % grid.ny) * strip
                strips.append(lax.dynamic_slice_in_dim(mats, start, strip, 2))
            parts.append(jnp.concatenate(strips, axis=2))
    return parts


def site_kernel(grid, site, last, strip, clicks_ref, *refs):
    nx, ny, nz = grid.nx, grid.ny, grid.nz
    mine, other, states = refs[:nx], refs[nx : 2 * nx], refs[2 * nx : 2 * nx + nz]
    outs = refs[2 * nx + nz : 2 * nx + nz + nx * ny]
    mat_ref, high_ref, low_ref, sems = refs[2 * nx + nz + nx * ny :]
    _, _, y, core = grid.here()
    owner = core == site % grid.cores
    for dx in range(nx):

        @pl.when(owner)
        def _():
            pltpu.make_async_copy(mine[dx], mat_ref.at[dx], sems.at[dx]).start()

        @pl.when(jnp.logical_not(owner))
        def _():
            pltpu.make_async_copy(other[dx], mat_ref.at[dx], sems.at[dx]).start()

    for d in range(nz):
        high, low = halves(states[d][...])
        high_ref[pl.ds(d * strip, strip), :] = high
        low_ref[pl.ds(d * strip, strip), :] = low
    chosen = clicks_ref[...] == 1
    rows = mat_ref.shape[2]
    cols = high_ref.shape[1] // ny
    for ex in range(nx):
        dx = (nx - ex) % nx
        pltpu.make_async_copy(mine[dx], mat_ref.at[dx], sems.at[dx]).wait()
        for ey in range(ny):
            to = lax.rem(y + ey, ny)
            out_ref = outs[ex * ny + ey]
            if last:
                picked = pl.ds(pl.multiple_of(to * cols, cols), cols)
                b = (high_ref[:, picked], low_ref[:, picked])
                for part in range(rows // strip):
                    at = pl.ds(part * strip, strip)
                    both = [dot3(halves(mat_ref[dx, o, at, :]), b) for o in range(2)]
                    out_ref[at, :] = jnp.where(clicks_ref[:, picked] == 1, both[1], both[0])
            else:
                at = pl.ds(pl.multiple_of(to * strip, strip), strip)
                b = (high_ref[...], low_ref[...])
                both = [dot3(halves(mat_ref[dx, o, at, :]), b) for o in range(2)]
                out_ref[...] = jnp.where(chosen, both[1], both[0])


def site_product(grid, site, last, clicks, mine, other, states):
    nx, ny, nz = grid.nx, grid.ny, grid.nz
    outcomes, rows, width = mine[0].shape
    strip, cols = states[0].shape
    shape = (rows, cols // ny) if last else (strip, cols)
    if strip % 128 == 0 and (cols // ny) % 128 == 0:
        vmem, hbm = pl.BlockSpec(memory_space=pltpu.VMEM), pl.BlockSpec(memory_space=pl.ANY)
        flops = 2 * 3 * outcomes * nx * rows * width * cols
        moved = 4 * (nx * outcomes * rows * width + width * cols + nx * rows * cols)
        return pl.pallas_call(
            functools.partial(site_kernel, grid, site, last, strip),
            out_shape=[jax.ShapeDtypeStruct(shape, jnp.float32)] * (nx * ny),
            in_specs=[vmem] + [hbm] * (2 * nx) + [vmem] * nz,
            out_specs=[vmem] * (nx * ny),
            scratch_shapes=[
                pltpu.VMEM((nx, outcomes, rows, width), jnp.float32),
                pltpu.VMEM((width, cols), jnp.bfloat16),
                pltpu.VMEM((width, cols), jnp.bfloat16),
                pltpu.SemaphoreType.DMA((nx,)),
            ],
            compiler_params=pltpu.CompilerParams(vmem_limit_bytes=32 * 1024 * 1024),
            cost_estimate=pl.CostEstimate(flops=flops, bytes_accessed=moved, transcendentals=0),
        )(clicks, *mine, *other, *states)
    _, _, y, core = grid.here()
    b = jnp.concatenate(states, axis=0)
    outs = []
    for ex in range(nx):
        dx = (nx - ex) % nx
        mat = jnp.where(core == site % grid.cores, mine[dx], other[dx])
        both = [jnp.dot(mat[o], b, precision=lax.Precision.HIGH, preferred_element_type=jnp.float32) for o in range(2)]
        picked = jnp.where(clicks == 1, both[1], both[0])
        for ey in range(ny):
            to = (y + ey) % ny
            if last:
                outs.append(lax.dynamic_slice_in_dim(picked, to * shape[1], shape[1], 1))
            else:
                outs.append(lax.dynamic_slice_in_dim(picked, to * shape[0], shape[0], 0))
    return outs


def local(left_start, site_mats, clicks):
    sites, bonds = lax.axis_size("site"), lax.axis_size("bond")
    grid = Grid(sites, bonds)
    nx, ny, nz, cores = grid.nx, grid.ny, grid.nz, grid.cores
    z, x, y, core = grid.here()
    rows = site_mats.shape[2]
    strip = rows // ny
    samples = left_start.shape[1]
    share = samples // sites

    def own_samples(value):
        blocks = [lax.dynamic_slice_in_dim(value, (yy * cores + core) * share, share, 1) for yy in range(ny)]
        return jnp.concatenate(blocks, axis=1)

    pieces = pack(grid, site_mats[0], rows, strip)

    def spread(which):
        got = {}
        for dx in range(nx):
            for dy in range(ny):
                piece = pieces[dx * ny + dy]
                got[dx, dy] = piece if dx == dy == 0 else grid.send(piece, dx=dx, dy=dy, cores=[which])
        return got

    def of_site(got, ys):
        mine = []
        for dx in range(nx):
            value = got[dx, 0]
            for dy in range(1, ny):
                value = jnp.where((y - ys) % ny == dy, got[dx, dy], value)
            mine.append(value)
        return mine

    state = own_samples(lax.dynamic_slice_in_dim(left_start, y * strip, strip, 0))
    gathered = [state] + [grid.send(state, dz=d) for d in range(1, nz)]
    own_clicks = {(0, 0): clicks}
    for dy in range(ny):
        for dcore in range(cores):
            if dy or dcore:
                own_clicks[dy, dcore] = grid.send(clicks, dy=dy, dcore=dcore)

    def clicks_of(site):
        value = own_clicks[0, 0]
        for (dy, dcore), got in own_clicks.items():
            hit = ((y - site // cores) % ny == dy) & ((core - site % cores) % cores == dcore)
            value = jnp.where(hit, got, value)
        return own_samples(value)

    spreads = [spread(which) for which in range(cores)]
    for site in range(sites):
        last = site == sites - 1
        which = site % cores
        mine = of_site(spreads[which], site // cores)
        other = [grid.send(value, dcore=1, cores=[which]) for value in mine]
        outs = site_product(grid, site, last, clicks_of(site), mine, other, gathered)
        state = outs[0]
        for ex in range(nx):
            for ey in range(ny):
                if ex or ey:
                    state = state + grid.send(outs[ex * ny + ey], dx=ex, dy=ey)
        if not last:
            gathered = [state] + [grid.send(state, dz=d) for d in range(1, nz)]
    return state


def solution(mesh):
    return jax.shard_map(
        local,
        mesh=mesh,
        in_specs=(P("bond", None), P("site", None, "bond", None), P("site", None)),
        out_specs=P("bond", "site"),
        check_vma=False,
    )
```

```python
import functools

import jax
import jax.numpy as jnp
from jax import lax
from jax.experimental import pallas as pl
from jax.experimental.pallas import tpu as pltpu
from jax.sharding import PartitionSpec as P


CLICK_ROWS = 8


class Grid:
    def __init__(self, sites, bonds, rows, samples):
        self.sites, self.bonds = sites, bonds
        self.cores = 2 if sites % 2 == 0 else 1
        self.ny = sites // self.cores
        self.nx = max(q for q in range(1, bonds + 1) if bonds % q == 0 and q * q <= bonds)
        self.nz = bonds // self.nx
        self.rows = rows
        self.strip = rows // self.ny
        self.width = self.strip * self.nz
        self.share = samples // sites
        self.cols = self.share * self.ny
        aligned = self.strip % 128 == 0 and self.share % 128 == 0
        self.kernels = aligned and self.cols == self.width and self.cores <= CLICK_ROWS

    def here(self):
        site, bond = lax.axis_index("site"), lax.axis_index("bond")
        return bond // self.nx, bond % self.nx, site // self.cores, site % self.cores

    def index(self, z, x, y, core):
        site = (y % self.ny) * self.cores + core % self.cores
        return site * self.bonds + (z % self.nz) * self.nx + x % self.nx

    def send(self, value, dz=0, dx=0, dy=0, dcore=0, across=0, cores=None):
        pairs = []
        for z in range(self.nz):
            for x in range(self.nx):
                for y in range(self.ny):
                    for core in range(self.cores) if cores is None else cores:
                        to = self.index((z ^ across) + dz, x + dx, y + dy, core + dcore)
                        pairs.append((self.index(z, x, y, core), to))
        return lax.ppermute(value, ("site", "bond"), pairs)

    def gather(self, state, relay=False):
        if self.nz & (self.nz - 1):
            return [state] + [self.send(state, dz=self.nz - d) for d in range(1, self.nz)]
        got = [state]
        for d in range(1, self.nz):
            got.append(self.send(got[d ^ 1], across=1) if relay and d & 1 else self.send(state, across=d))
        return got

    def gathered_from(self, z):
        if self.nz & (self.nz - 1):
            return [lax.rem(z + d, self.nz) for d in range(self.nz)]
        return [z ^ d for d in range(self.nz)]


def halves(value):
    high = value.astype(jnp.bfloat16)
    low = (value - high.astype(jnp.float32)).astype(jnp.bfloat16)
    return high, low


def dot3(a, b):
    dot = functools.partial(jnp.dot, preferred_element_type=jnp.float32)
    return dot(a[0], b[0]) + (dot(a[0], b[1]) + dot(a[1], b[0]))


def pack_kernel(grid, clicks_ref, mats_ref, left_ref, *refs):
    nx, ny, nz, cores, rows, strip, share = grid.nx, grid.ny, grid.nz, grid.cores, grid.rows, grid.strip, grid.share
    piece_refs, state_ref = refs[: nx * ny], refs[nx * ny]
    clicks_held_ref, held_ref, left_held_ref, clicks_sem, in_sems, out_sems, left_sems, state_sem = refs[nx * ny + 1 :]
    _, x, y, core = grid.here()
    clicks_copy = pltpu.make_async_copy(clicks_ref, clicks_held_ref, clicks_sem)
    clicks_copy.start()
    order = [(dx, dy) for dx in reversed(range(nx)) for dy in reversed(range(ny))]
    into = {}
    for dx, dy in order:
        e = dx * ny + dy
        into[e] = []
        for zz in range(nz):
            start = zz * nx * rows + lax.rem(x + dx, nx) * rows + lax.rem(y + dy, ny) * strip
            columns = pl.ds(pl.multiple_of(start, strip), strip)
            for o in range(2):
                target = held_ref.at[e, pl.ds(o * rows, rows), pl.ds(zz * strip, strip)]
                into[e].append(pltpu.make_async_copy(mats_ref.at[o, :, columns], target, in_sems.at[e, zz, o]))
        for copy in into[e]:
            copy.start()
    states = []
    for yy in range(ny):
        start = pl.multiple_of((yy * cores + core) * share, share)
        source = left_ref.at[pl.ds(pl.multiple_of(y * strip, strip), strip), pl.ds(start, share)]
        states.append(pltpu.make_async_copy(source, left_held_ref.at[:, pl.ds(yy * share, share)], left_sems.at[yy]))
    for copy in states:
        copy.start()
    clicks_copy.wait()
    for e in range(nx * ny):
        held_ref[e, 2 * rows :, :] = jnp.zeros((CLICK_ROWS, grid.width), jnp.float32)
        for c in range(cores):
            for yy in range(ny):
                start = (yy * cores + c) * share
                value = clicks_held_ref[:, start : start + share].astype(jnp.float32)
                held_ref[e, 2 * rows + c : 2 * rows + c + 1, yy * share : (yy + 1) * share] = value
    outward = []
    for dx, dy in order:
        e = dx * ny + dy
        for copy in into[e]:
            copy.wait()
        outward.append(pltpu.make_async_copy(held_ref.at[e], piece_refs[e], out_sems.at[e]))
        outward[-1].start()
    for copy in states:
        copy.wait()
    outward.append(pltpu.make_async_copy(left_held_ref, state_ref, state_sem))
    outward[-1].start()
    for copy in outward:
        copy.wait()


def own_samples(grid, value):
    core = grid.here()[3]
    starts = [(yy * grid.cores + core) * grid.share for yy in range(grid.ny)]
    return jnp.concatenate([lax.dynamic_slice_in_dim(value, start, grid.share, 1) for start in starts], axis=1)


def pack(grid, clicks, mats, left):
    nx, ny, nz, rows, strip = grid.nx, grid.ny, grid.nz, grid.rows, grid.strip
    if grid.kernels:
        hbm = pl.BlockSpec(memory_space=pltpu.HBM)
        tall = 2 * rows + CLICK_ROWS
        out = pl.pallas_call(
            functools.partial(pack_kernel, grid),
            out_shape=[jax.ShapeDtypeStruct((tall, grid.width), jnp.float32)] * (nx * ny)
            + [jax.ShapeDtypeStruct((strip, grid.cols), jnp.float32)],
            in_specs=[hbm] * 3,
            out_specs=[hbm] * (nx * ny + 1),
            scratch_shapes=[
                pltpu.VMEM(clicks.shape, jnp.int32),
                pltpu.VMEM((nx * ny, tall, grid.width), jnp.float32),
                pltpu.VMEM((strip, grid.cols), jnp.float32),
                pltpu.SemaphoreType.DMA,
                pltpu.SemaphoreType.DMA((nx * ny, nz, 2)),
                pltpu.SemaphoreType.DMA((nx * ny,)),
                pltpu.SemaphoreType.DMA((ny,)),
                pltpu.SemaphoreType.DMA,
            ],
            compiler_params=pltpu.CompilerParams(vmem_limit_bytes=57 * 1024 * 1024),
            cost_estimate=pl.CostEstimate(flops=0, bytes_accessed=2 * mats.size * 4, transcendentals=0),
        )(clicks, mats, left)
        return out[: nx * ny], out[nx * ny]
    _, x, y, _ = grid.here()
    pieces = []
    for dx in range(nx):
        for dy in range(ny):
            strips = []
            for zz in range(nz):
                start = zz * nx * rows + ((x + dx) % nx) * rows + ((y + dy) % ny) * strip
                strips.append(lax.dynamic_slice_in_dim(mats, start, strip, 2))
            pieces.append(jnp.concatenate(strips, axis=2).reshape(2 * rows, grid.width))
    return pieces, own_samples(grid, lax.dynamic_slice_in_dim(left, y * strip, strip, 0))


def collect_kernel(grid, site, keys, *refs):
    n = len(keys)
    pieces, (out_ref, held_ref, in_sems, out_sems) = dict(zip(keys, refs[:n])), refs[-4:]
    y = grid.here()[2]
    behind = lax.rem(y + grid.ny - site // grid.cores, grid.ny)
    for dx, dy in keys:

        @pl.when(behind == dy)
        def _():
            pltpu.make_async_copy(pieces[dx, dy], held_ref.at[dx], in_sems.at[dx]).start()

    outward = []
    for dx in range(grid.nx):
        pltpu.make_async_copy(pieces[dx, 0], held_ref.at[dx], in_sems.at[dx]).wait()
        outward.append(pltpu.make_async_copy(held_ref.at[dx], out_ref.at[dx], out_sems.at[dx]))
        outward[-1].start()
    for copy in outward:
        copy.wait()


def collect(grid, site, pieces, token):
    nx = grid.nx
    tall, width = pieces[0, 0].shape
    if grid.kernels:
        hbm, fixed = pl.BlockSpec(memory_space=pl.ANY), pl.BlockSpec(memory_space=pltpu.HBM)
        return pl.pallas_call(
            functools.partial(collect_kernel, grid, site, tuple(pieces)),
            out_shape=jax.ShapeDtypeStruct((nx, tall, width), jnp.float32),
            in_specs=[fixed if key == (0, 0) else hbm for key in pieces] + [hbm] * len(token),
            out_specs=hbm,
            scratch_shapes=[
                pltpu.VMEM((nx, tall, width), jnp.float32),
                pltpu.SemaphoreType.DMA((nx,)),
                pltpu.SemaphoreType.DMA((nx,)),
            ],
            compiler_params=pltpu.CompilerParams(vmem_limit_bytes=32 * 1024 * 1024),
            cost_estimate=pl.CostEstimate(flops=0, bytes_accessed=8 * nx * tall * width, transcendentals=0),
        )(*pieces.values(), *token)
    behind = (grid.here()[2] - site // grid.cores) % grid.ny
    rows = []
    for dx in range(nx):
        value = pieces[dx, 0]
        for dy in range(1, grid.ny):
            value = jnp.where(behind == dy, pieces[dx, dy], value)
        rows.append(value)
    return jnp.stack(rows)


def site_kernel(grid, site, last, tokens, mine_ref, other_ref, *refs):
    nx, ny, nz, rows, strip, share = grid.nx, grid.ny, grid.nz, grid.rows, grid.strip, grid.share
    states, refs = refs[:nz], refs[nz + tokens :]
    outs = refs[: nx * ny]
    mat_ref, state_ref, high_ref, low_ref, sems, state_sems = refs[nx * ny :]
    z, _, y, core = grid.here()
    owner = core == site % grid.cores
    inward = []
    for n, source in enumerate(grid.gathered_from(z)):
        at = pl.ds(pl.multiple_of(source * strip, strip), strip)
        inward.append(pltpu.make_async_copy(states[n], state_ref.at[at], state_sems.at[n]))
        inward[-1].start()

    @pl.when(owner)
    def _():
        for dx in range(nx):
            pltpu.make_async_copy(mine_ref.at[dx], mat_ref.at[dx], sems.at[dx]).start()

    @pl.when(jnp.logical_not(owner))
    def _():
        for dx in range(nx):
            pltpu.make_async_copy(other_ref.at[dx], mat_ref.at[dx], sems.at[dx]).start()

    for copy in inward:
        copy.wait()
    high_ref[...], low_ref[...] = halves(state_ref[...])
    for ex in range(nx):
        dx = (nx - ex) % nx
        pltpu.make_async_copy(mine_ref.at[dx], mat_ref.at[dx], sems.at[dx]).wait()
        if ex == 0:
            clicks = mat_ref[0, 2 * rows : 2 * rows + CLICK_ROWS, :]
            row = lax.broadcasted_iota(jnp.int32, clicks.shape, 0)
            clicks = jnp.sum(jnp.where(row == core, clicks, 0.0), axis=0, keepdims=True)
        for ey in range(ny):
            to = lax.rem(y + ey, ny)
            out_ref = outs[ex * ny + ey]
            if last:
                columns = pl.ds(pl.multiple_of(to * share, share), share)
                b = (high_ref[:, columns], low_ref[:, columns])
                picked = jnp.zeros((1, share), jnp.float32)
                for yy in range(ny):
                    picked = jnp.where(to == yy, clicks[:, yy * share : (yy + 1) * share], picked)
                both = [dot3(halves(mat_ref[dx, o * rows : (o + 1) * rows, :]), b) for o in range(2)]
                out_ref[...] = jnp.where(picked == 1, both[1], both[0])
            else:
                at = pl.multiple_of(to * strip, strip)
                b = (high_ref[...], low_ref[...])
                both = [dot3(halves(mat_ref[dx, pl.ds(o * rows + at, strip), :]), b) for o in range(2)]
                out_ref[...] = jnp.where(clicks == 1, both[1], both[0])


def site_product(grid, site, clicks, mine, other, states, token=()):
    nx, ny, nz, rows, width, cols = grid.nx, grid.ny, grid.nz, grid.rows, grid.width, grid.cols
    last = site == grid.sites - 1
    shape = (rows, grid.share) if last else (grid.strip, cols)
    if grid.kernels:
        vmem, hbm = pl.BlockSpec(memory_space=pltpu.VMEM), pl.BlockSpec(memory_space=pl.ANY)
        fixed = pl.BlockSpec(memory_space=pltpu.HBM)
        tall = mine.shape[1]
        flops = 2 * 3 * 2 * nx * rows * width * cols
        moved = 4 * (nx * tall * width + width * cols + nx * rows * cols)
        return pl.pallas_call(
            functools.partial(site_kernel, grid, site, last, len(token)),
            out_shape=[jax.ShapeDtypeStruct(shape, jnp.float32)] * (nx * ny),
            in_specs=[hbm] * 2 + [fixed if site == 0 else hbm] + [hbm] * (nz - 1 + len(token)),
            out_specs=[vmem] * (nx * ny),
            scratch_shapes=[
                pltpu.VMEM((nx, tall, width), jnp.float32),
                pltpu.VMEM((width, cols), jnp.float32),
                pltpu.VMEM((width, cols), jnp.bfloat16),
                pltpu.VMEM((width, cols), jnp.bfloat16),
                pltpu.SemaphoreType.DMA((nx,)),
                pltpu.SemaphoreType.DMA((nz,)),
            ],
            compiler_params=pltpu.CompilerParams(vmem_limit_bytes=32 * 1024 * 1024),
            cost_estimate=pl.CostEstimate(flops=flops, bytes_accessed=moved, transcendentals=0),
        )(mine, other, *states, *token)
    z, _, y, core = grid.here()
    whole = jnp.zeros((width, cols), jnp.float32)
    for value, source in zip(states, grid.gathered_from(z)):
        whole = lax.dynamic_update_slice_in_dim(whole, value, source * grid.strip, 0)
    outs = []
    for ex in range(nx):
        dx = (nx - ex) % nx
        mat = jnp.where(core == site % grid.cores, mine[dx], other[dx])
        both = jnp.dot(mat, whole, precision=lax.Precision.HIGH, preferred_element_type=jnp.float32)
        picked = jnp.where(clicks == 1, both[rows:], both[:rows])
        for ey in range(ny):
            axis = 1 if last else 0
            outs.append(lax.dynamic_slice_in_dim(picked, ((y + ey) % ny) * shape[axis], shape[axis], axis))
    return outs


def local(left_start, site_mats, clicks):
    sites, bonds = lax.axis_size("site"), lax.axis_size("bond")
    grid = Grid(sites, bonds, site_mats.shape[2], left_start.shape[1])
    nx, ny, nz, cores = grid.nx, grid.ny, grid.nz, grid.cores
    _, _, y, core = grid.here()
    pieces, state = pack(grid, clicks, site_mats[0], left_start)
    shifts = [(dx, dy) for dx in range(nx) for dy in range(ny)]

    own_clicks = {}
    if not grid.kernels:
        for dy in range(ny):
            for dcore in range(cores):
                own_clicks[dy, dcore] = grid.send(clicks, dy=dy, dcore=dcore) if dy or dcore else clicks

    def clicks_of(site):
        value = clicks
        for (dy, dcore), got in own_clicks.items():
            hit = ((y - site // cores) % ny == dy) & ((core - site % cores) % cores == dcore)
            value = jnp.where(hit, got, value)
        return own_samples(grid, value)

    def spread(which, pieces, some):
        return {(dx, dy): grid.send(pieces[dx * ny + dy], dx=dx, dy=dy, cores=[which]) for dx, dy in some}

    straight = [(dx, dy) for dx, dy in shifts[1:] if not (dx and dy)]
    oblique = [(dx, dy) for dx, dy in shifts if dx and dy]
    spreads = [{(0, 0): pieces[0]} for _ in range(max(cores, 2))]
    spreads[0].update(spread(0, pieces, shifts[:0:-1]))
    sides = {}

    def sides_of(site, token):
        mine = collect(grid, site, spreads[site % cores], token)
        sides[site] = mine, grid.send(mine, dcore=1, cores=[site % cores])

    for site in range(sites):
        gathered = grid.gather(state, relay=True)
        if site < cores - 1:
            gathered[-1], later = lax.optimization_barrier((gathered[-1], pieces))
            spreads[site + 1].update(spread(site + 1, later, straight))
        token = gathered if site == 0 else gathered[1:3]
        if 0 < site < sites - 1:
            sides_of(site + 1, token)
            token = sides[site + 1][:1]
        if site not in sides:
            sides_of(site, token)
        mine, other = sides[site]
        token = list(spreads[1].values())[1:] if site == 0 else []
        outs = site_product(grid, site, clicks_of(site), mine, other, gathered, token)
        state = outs[0]
        for e, (ex, ey) in enumerate(shifts):
            if e:
                state = state + grid.send(outs[e], dx=ex, dy=ey)
        if site < cores - 1:
            state, later = lax.optimization_barrier((state, pieces))
            spreads[site + 1].update(spread(site + 1, later, oblique))
    return state


def solution(mesh):
    return jax.shard_map(
        local,
        mesh=mesh,
        in_specs=(P("bond", None), P("site", None, "bond", None), P("site", None)),
        out_specs=P("bond", "site"),
        check_vma=False,
    )
```

```python
import functools

import jax
import jax.numpy as jnp
from jax import lax
from jax.experimental import pallas as pl
from jax.experimental.pallas import tpu as pltpu
from jax.sharding import PartitionSpec as P


CLICK_ROWS = 8
PACK_VMEM = 48 * 1024 * 1024
RELAY = (True, True, True)


class Grid:
    def __init__(self, sites, bonds, rows, samples):
        self.sites, self.bonds = sites, bonds
        self.cores = 2 if sites % 2 == 0 else 1
        self.ny = sites // self.cores
        self.nx = max(q for q in range(1, bonds + 1) if bonds % q == 0 and q * q <= bonds)
        self.nz = bonds // self.nx
        self.rows = rows
        self.strip = rows // self.ny
        self.width = self.strip * self.nz
        self.share = samples // sites
        self.cols = self.share * self.ny
        aligned = self.strip % 128 == 0 and self.share % 128 == 0
        self.kernels = aligned and self.cols == self.width and self.cores <= CLICK_ROWS

    def here(self):
        site, bond = lax.axis_index("site"), lax.axis_index("bond")
        return bond // self.nx, bond % self.nx, site // self.cores, site % self.cores

    def index(self, z, x, y, core):
        site = (y % self.ny) * self.cores + core % self.cores
        return site * self.bonds + (z % self.nz) * self.nx + x % self.nx

    def send(self, value, dz=0, dx=0, dy=0, dcore=0, across=0, cores=None):
        pairs = []
        for z in range(self.nz):
            for x in range(self.nx):
                for y in range(self.ny):
                    for core in range(self.cores) if cores is None else cores:
                        to = self.index((z ^ across) + dz, x + dx, y + dy, core + dcore)
                        pairs.append((self.index(z, x, y, core), to))
        return lax.ppermute(value, ("site", "bond"), pairs)

    def gather(self, state, relay=False):
        if self.nz & (self.nz - 1):
            return [state] + [self.send(state, dz=self.nz - d) for d in range(1, self.nz)]
        got = [state]
        for d in range(1, self.nz):
            got.append(self.send(got[d ^ 1], across=1) if relay and d & 1 else self.send(state, across=d))
        return got

    def gathered_from(self, z):
        if self.nz & (self.nz - 1):
            return [lax.rem(z + d, self.nz) for d in range(self.nz)]
        return [z ^ d for d in range(self.nz)]


def halves(value):
    high = value.astype(jnp.bfloat16)
    low = (value - high.astype(jnp.float32)).astype(jnp.bfloat16)
    return high, low


def dot3(a, b):
    dot = functools.partial(jnp.dot, preferred_element_type=jnp.float32)
    return dot(a[0], b[0]) + (dot(a[0], b[1]) + dot(a[1], b[0]))


def pack_kernel(grid, clicks_ref, mats_ref, left_ref, *refs):
    nx, ny, nz, cores, rows, strip, share = grid.nx, grid.ny, grid.nz, grid.cores, grid.rows, grid.strip, grid.share
    piece_refs, state_ref = refs[: nx * ny], refs[nx * ny]
    clicks_held_ref, clicks_sem, in_sems, left_sems = refs[nx * ny + 1 :]
    _, x, y, core = grid.here()
    clicks_copy = pltpu.make_async_copy(clicks_ref, clicks_held_ref, clicks_sem)
    clicks_copy.start()
    order = [(dx, dy) for dx in reversed(range(nx)) for dy in reversed(range(ny))]
    into = {}
    for dx, dy in order:
        e = dx * ny + dy
        into[e] = []
        for zz in range(nz):
            start = zz * nx * rows + lax.rem(x + dx, nx) * rows + lax.rem(y + dy, ny) * strip
            columns = pl.ds(pl.multiple_of(start, strip), strip)
            for o in range(2):
                target = piece_refs[e].at[pl.ds(o * rows, rows), pl.ds(zz * strip, strip)]
                into[e].append(pltpu.make_async_copy(mats_ref.at[o, :, columns], target, in_sems.at[e, zz, o]))
        for copy in into[e]:
            copy.start()
    states = []
    for yy in range(ny):
        start = pl.multiple_of((yy * cores + core) * share, share)
        source = left_ref.at[pl.ds(pl.multiple_of(y * strip, strip), strip), pl.ds(start, share)]
        states.append(pltpu.make_async_copy(source, state_ref.at[:, pl.ds(yy * share, share)], left_sems.at[yy]))
    for copy in states:
        copy.start()
    clicks_copy.wait()
    for piece_ref in piece_refs:
        piece_ref[2 * rows :, :] = jnp.zeros((CLICK_ROWS, grid.width), jnp.float32)
        for c in range(cores):
            for yy in range(ny):
                start = (yy * cores + c) * share
                value = clicks_held_ref[:, start : start + share].astype(jnp.float32)
                piece_ref[2 * rows + c : 2 * rows + c + 1, yy * share : (yy + 1) * share] = value
    for copy in sum(into.values(), states):
        copy.wait()


def own_samples(grid, value):
    core = grid.here()[3]
    starts = [(yy * grid.cores + core) * grid.share for yy in range(grid.ny)]
    return jnp.concatenate([lax.dynamic_slice_in_dim(value, start, grid.share, 1) for start in starts], axis=1)


def pack(grid, clicks, mats, left):
    nx, ny, nz, rows, strip = grid.nx, grid.ny, grid.nz, grid.rows, grid.strip
    if grid.kernels:
        vmem, hbm = pl.BlockSpec(memory_space=pltpu.VMEM), pl.BlockSpec(memory_space=pltpu.HBM)
        tall = 2 * rows + CLICK_ROWS
        out = pl.pallas_call(
            functools.partial(pack_kernel, grid),
            out_shape=[jax.ShapeDtypeStruct((tall, grid.width), jnp.float32)] * (nx * ny)
            + [jax.ShapeDtypeStruct((strip, grid.cols), jnp.float32)],
            in_specs=[hbm] * 3,
            out_specs=[vmem] * (nx * ny + 1),
            scratch_shapes=[
                pltpu.VMEM(clicks.shape, jnp.int32),
                pltpu.SemaphoreType.DMA,
                pltpu.SemaphoreType.DMA((nx * ny, nz, 2)),
                pltpu.SemaphoreType.DMA((ny,)),
            ],
            compiler_params=pltpu.CompilerParams(vmem_limit_bytes=PACK_VMEM),
            cost_estimate=pl.CostEstimate(flops=0, bytes_accessed=2 * mats.size * 4, transcendentals=0),
        )(clicks, mats, left)
        return out[: nx * ny], out[nx * ny]
    _, x, y, _ = grid.here()
    pieces = []
    for dx in range(nx):
        for dy in range(ny):
            strips = []
            for zz in range(nz):
                start = zz * nx * rows + ((x + dx) % nx) * rows + ((y + dy) % ny) * strip
                strips.append(lax.dynamic_slice_in_dim(mats, start, strip, 2))
            pieces.append(jnp.concatenate(strips, axis=2).reshape(2 * rows, grid.width))
    return pieces, own_samples(grid, lax.dynamic_slice_in_dim(left, y * strip, strip, 0))


def collect_kernel(grid, sites, keys, *refs):
    pieces, (out_ref, held_ref, in_sems, out_sems) = dict(zip(keys, refs)), refs[-4:]
    _, _, y, core = grid.here()

    @pl.when(core == sites[0] % grid.cores)
    def _():
        for k, site in enumerate(sites):
            behind = lax.rem(y + grid.ny - site // grid.cores, grid.ny)
            for dx, dy in keys:

                @pl.when(behind == dy)
                def _():
                    pltpu.make_async_copy(pieces[dx, dy], held_ref.at[k, dx], in_sems.at[k, dx]).start()

        outward = []
        for k in range(len(sites)):
            for dx in range(grid.nx):
                pltpu.make_async_copy(refs[0], held_ref.at[k, dx], in_sems.at[k, dx]).wait()
                outward.append(pltpu.make_async_copy(held_ref.at[k, dx], out_ref.at[k, dx], out_sems.at[k, dx]))
                outward[-1].start()
        for copy in outward:
            copy.wait()


def collect(grid, sites, pieces, token=()):
    nx = grid.nx
    keys = tuple(pieces)
    tall, width = pieces[0, 0].shape
    if grid.kernels:
        hbm = pl.BlockSpec(memory_space=pl.ANY)
        shape = (len(sites), nx, tall, width)
        operands = list(pieces.values()) + list(token)
        return pl.pallas_call(
            functools.partial(collect_kernel, grid, tuple(sites), keys),
            out_shape=jax.ShapeDtypeStruct(shape, jnp.float32),
            in_specs=[hbm] * len(operands),
            out_specs=hbm,
            scratch_shapes=[
                pltpu.VMEM(shape, jnp.float32),
                pltpu.SemaphoreType.DMA(shape[:2]),
                pltpu.SemaphoreType.DMA(shape[:2]),
            ],
            compiler_params=pltpu.CompilerParams(vmem_limit_bytes=32 * 1024 * 1024),
            cost_estimate=pl.CostEstimate(flops=0, bytes_accessed=8 * len(sites) * nx * tall * width, transcendentals=0),
        )(*operands)
    mats = []
    for site in sites:
        behind = (grid.here()[2] - site // grid.cores) % grid.ny
        for dx in range(nx):
            value = pieces[dx, 0]
            for dy in range(1, grid.ny):
                value = jnp.where(behind == dy, pieces[dx, dy], value)
            mats.append(value)
    return jnp.stack(mats).reshape(len(sites), nx, tall, width)


def site_kernel(grid, site, last, tokens, *refs):
    nx, ny, nz, rows, strip, share = grid.nx, grid.ny, grid.nz, grid.rows, grid.strip, grid.share
    mats, refs = refs[: grid.cores], refs[grid.cores :]
    states, refs = refs[:nz], refs[nz + tokens :]
    outs = refs[: nx * ny]
    mat_ref, state_ref, high_ref, low_ref, sems, state_sems = refs[nx * ny :]
    z, _, y, core = grid.here()
    place = site // grid.cores
    inward = []
    for n, source in enumerate(grid.gathered_from(z)):
        at = pl.ds(pl.multiple_of(source * strip, strip), strip)
        inward.append(pltpu.make_async_copy(states[n], state_ref.at[at], state_sems.at[n]))
        inward[-1].start()

    for role, ref in enumerate(mats):

        @pl.when(core == role)
        def _():
            for dx in range(nx):
                pltpu.make_async_copy(ref.at[place, dx], mat_ref.at[dx], sems.at[dx]).start()

    for copy in inward:
        copy.wait()
    high_ref[...], low_ref[...] = halves(state_ref[...])
    for ex in range(nx):
        dx = (nx - ex) % nx
        pltpu.make_async_copy(mats[0].at[place, dx], mat_ref.at[dx], sems.at[dx]).wait()
        if ex == 0:
            clicks = mat_ref[0, 2 * rows : 2 * rows + CLICK_ROWS, :]
            row = lax.broadcasted_iota(jnp.int32, clicks.shape, 0)
            clicks = jnp.sum(jnp.where(row == core, clicks, 0.0), axis=0, keepdims=True)
        for ey in range(ny):
            to = lax.rem(y + ey, ny)
            out_ref = outs[ex * ny + ey]
            if last:
                columns = pl.ds(pl.multiple_of(to * share, share), share)
                b = (high_ref[:, columns], low_ref[:, columns])
                picked = jnp.zeros((1, share), jnp.float32)
                for yy in range(ny):
                    picked = jnp.where(to == yy, clicks[:, yy * share : (yy + 1) * share], picked)
                both = [dot3(halves(mat_ref[dx, o * rows : (o + 1) * rows, :]), b) for o in range(2)]
                out_ref[...] = jnp.where(picked == 1, both[1], both[0])
            else:
                at = pl.multiple_of(to * strip, strip)
                b = (high_ref[...], low_ref[...])
                both = [dot3(halves(mat_ref[dx, pl.ds(o * rows + at, strip), :]), b) for o in range(2)]
                out_ref[...] = jnp.where(clicks == 1, both[1], both[0])


def site_product(grid, site, clicks, mats, states, token=()):
    nx, ny, nz, rows, width, cols = grid.nx, grid.ny, grid.nz, grid.rows, grid.width, grid.cols
    last = site == grid.sites - 1
    shape = (rows, grid.share) if last else (grid.strip, cols)
    if grid.kernels:
        vmem, hbm = pl.BlockSpec(memory_space=pltpu.VMEM), pl.BlockSpec(memory_space=pl.ANY)
        tall = grid.rows * 2 + CLICK_ROWS
        flops = 2 * 3 * 2 * nx * rows * width * cols
        moved = 4 * (nx * tall * width + width * cols + nx * rows * cols)
        return pl.pallas_call(
            functools.partial(site_kernel, grid, site, last, len(token)),
            out_shape=[jax.ShapeDtypeStruct(shape, jnp.float32)] * (nx * ny),
            in_specs=[hbm] * (len(mats) + nz + len(token)),
            out_specs=[vmem] * (nx * ny),
            scratch_shapes=[
                pltpu.VMEM((nx, tall, width), jnp.float32),
                pltpu.VMEM((width, cols), jnp.float32),
                pltpu.VMEM((width, cols), jnp.bfloat16),
                pltpu.VMEM((width, cols), jnp.bfloat16),
                pltpu.SemaphoreType.DMA((nx,)),
                pltpu.SemaphoreType.DMA((nz,)),
            ],
            compiler_params=pltpu.CompilerParams(vmem_limit_bytes=32 * 1024 * 1024),
            cost_estimate=pl.CostEstimate(flops=flops, bytes_accessed=moved, transcendentals=0),
        )(*mats, *states, *token)
    z, _, y, core = grid.here()
    whole = jnp.zeros((width, cols), jnp.float32)
    for value, source in zip(states, grid.gathered_from(z)):
        whole = lax.dynamic_update_slice_in_dim(whole, value, source * grid.strip, 0)
    outs = []
    for ex in range(nx):
        dx = (nx - ex) % nx
        mat = 0
        for role, value in enumerate(mats):
            mat = jnp.where(core == role, value[site // grid.cores, dx], mat)
        both = jnp.dot(mat, whole, precision=lax.Precision.HIGH, preferred_element_type=jnp.float32)
        picked = jnp.where(clicks == 1, both[rows:], both[:rows])
        for ey in range(ny):
            axis = 1 if last else 0
            outs.append(lax.dynamic_slice_in_dim(picked, ((y + ey) % ny) * shape[axis], shape[axis], axis))
    return outs


def local(left_start, site_mats, clicks):
    sites, bonds = lax.axis_size("site"), lax.axis_size("bond")
    grid = Grid(sites, bonds, site_mats.shape[2], left_start.shape[1])
    nx, ny, nz, cores = grid.nx, grid.ny, grid.nz, grid.cores
    _, _, y, core = grid.here()
    pieces, state = pack(grid, clicks, site_mats[0], left_start)
    shifts = [(dx, dy) for dx in range(nx) for dy in range(ny)]

    own_clicks = {}
    if not grid.kernels:
        for dy in range(ny):
            for dcore in range(cores):
                own_clicks[dy, dcore] = grid.send(clicks, dy=dy, dcore=dcore) if dy or dcore else clicks

    def clicks_of(site):
        value = clicks
        for (dy, dcore), got in own_clicks.items():
            hit = ((y - site // cores) % ny == dy) & ((core - site % cores) % cores == dcore)
            value = jnp.where(hit, got, value)
        return own_samples(grid, value)

    def spread(which, pieces):
        got = {(dx, dy): grid.send(pieces[dx * ny + dy], dx=dx, dy=dy, cores=[which]) for dx, dy in shifts[:0:-1]}
        return {(0, 0): pieces[0], **got}

    mats = []
    for site in range(sites):
        gathered = grid.gather(state, relay=RELAY[min(site, 2)])
        token = []
        if site == 0:
            for which in range(cores):
                if which:
                    gathered[-1], later = lax.optimization_barrier((gathered[-1], pieces))
                mine = collect(grid, range(which, sites, cores), spread(which, later if which else pieces), gathered)
                others = [grid.send(mine, dcore=d, cores=[which]) for d in range(1, cores)]
                mats.append([([mine] + others)[(role - which) % cores] for role in range(cores)])
                token += [mine] if which else []
        outs = site_product(grid, site, clicks_of(site), mats[site % cores], gathered, token)
        state = outs[0]
        for ex, ey in shifts[:0:-1]:
            state = state + grid.send(outs[ex * ny + ey], dx=ex, dy=ey)
    return state


def solution(mesh):
    return jax.shard_map(
        local,
        mesh=mesh,
        in_specs=(P("bond", None), P("site", None, "bond", None), P("site", None)),
        out_specs=P("bond", "site"),
        check_vma=False,
    )
```

```python
import functools

import jax
import jax.numpy as jnp
from jax import lax
from jax.experimental import pallas as pl
from jax.experimental.pallas import tpu as pltpu
from jax.sharding import PartitionSpec as P


CLICK_ROWS = 8
PACK_VMEM = 48 * 1024 * 1024
RELAY = (True, True, False, True)


class Grid:
    def __init__(self, sites, bonds, rows, samples):
        self.sites, self.bonds = sites, bonds
        self.cores = 2 if sites % 2 == 0 else 1
        self.ny = sites // self.cores
        self.nx = max(q for q in range(1, bonds + 1) if bonds % q == 0 and q * q <= bonds)
        self.nz = bonds // self.nx
        self.rows = rows
        self.strip = rows // self.ny
        self.width = self.strip * self.nz
        self.share = samples // sites
        self.cols = self.share * self.ny
        aligned = self.strip % 128 == 0 and self.share % 128 == 0
        self.kernels = aligned and self.cols == self.width and self.cores <= CLICK_ROWS

    def here(self):
        site, bond = lax.axis_index("site"), lax.axis_index("bond")
        return bond // self.nx, bond % self.nx, site // self.cores, site % self.cores

    def index(self, z, x, y, core):
        site = (y % self.ny) * self.cores + core % self.cores
        return site * self.bonds + (z % self.nz) * self.nx + x % self.nx

    def send(self, value, dz=0, dx=0, dy=0, dcore=0, across=0, cores=None):
        pairs = []
        for z in range(self.nz):
            for x in range(self.nx):
                for y in range(self.ny):
                    for core in range(self.cores) if cores is None else cores:
                        to = self.index((z ^ across) + dz, x + dx, y + dy, core + dcore)
                        pairs.append((self.index(z, x, y, core), to))
        return lax.ppermute(value, ("site", "bond"), pairs)

    def gather(self, state, relay=False):
        if self.nz & (self.nz - 1):
            return [state] + [self.send(state, dz=self.nz - d) for d in range(1, self.nz)]
        got = [state]
        for d in range(1, self.nz):
            got.append(self.send(got[d ^ 1], across=1) if relay and d & 1 else self.send(state, across=d))
        return got

    def gathered_from(self, z):
        if self.nz & (self.nz - 1):
            return [lax.rem(z + d, self.nz) for d in range(self.nz)]
        return [z ^ d for d in range(self.nz)]


def halves(value):
    high = value.astype(jnp.bfloat16)
    low = (value - high.astype(jnp.float32)).astype(jnp.bfloat16)
    return high, low


def dot3(a, b):
    dot = functools.partial(jnp.dot, preferred_element_type=jnp.float32)
    return dot(a[0], b[0]) + (dot(a[0], b[1]) + dot(a[1], b[0]))


def pack_kernel(grid, clicks_ref, mats_ref, left_ref, *refs):
    nx, ny, nz, cores, rows, strip, share = grid.nx, grid.ny, grid.nz, grid.cores, grid.rows, grid.strip, grid.share
    piece_refs, state_ref = refs[: nx * ny], refs[nx * ny]
    clicks_held_ref, clicks_sem, in_sems, left_sems = refs[nx * ny + 1 :]
    _, x, y, core = grid.here()
    clicks_copy = pltpu.make_async_copy(clicks_ref, clicks_held_ref, clicks_sem)
    clicks_copy.start()
    order = [(dx, dy) for dx in reversed(range(nx)) for dy in reversed(range(ny))]
    into = {}
    for dx, dy in order:
        e = dx * ny + dy
        into[e] = []
        for zz in range(nz):
            start = zz * nx * rows + lax.rem(x + dx, nx) * rows + lax.rem(y + dy, ny) * strip
            columns = pl.ds(pl.multiple_of(start, strip), strip)
            for o in range(2):
                target = piece_refs[e].at[pl.ds(o * rows, rows), pl.ds(zz * strip, strip)]
                into[e].append(pltpu.make_async_copy(mats_ref.at[o, :, columns], target, in_sems.at[e, zz, o]))
        for copy in into[e]:
            copy.start()
    states = []
    for yy in range(ny):
        start = pl.multiple_of((yy * cores + core) * share, share)
        source = left_ref.at[pl.ds(pl.multiple_of(y * strip, strip), strip), pl.ds(start, share)]
        states.append(pltpu.make_async_copy(source, state_ref.at[:, pl.ds(yy * share, share)], left_sems.at[yy]))
    for copy in states:
        copy.start()
    clicks_copy.wait()
    for piece_ref in piece_refs:
        piece_ref[2 * rows :, :] = jnp.zeros((CLICK_ROWS, grid.width), jnp.float32)
        for c in range(cores):
            for yy in range(ny):
                start = (yy * cores + c) * share
                value = clicks_held_ref[:, start : start + share].astype(jnp.float32)
                piece_ref[2 * rows + c : 2 * rows + c + 1, yy * share : (yy + 1) * share] = value
    for copy in sum(into.values(), states):
        copy.wait()


def own_samples(grid, value):
    core = grid.here()[3]
    starts = [(yy * grid.cores + core) * grid.share for yy in range(grid.ny)]
    return jnp.concatenate([lax.dynamic_slice_in_dim(value, start, grid.share, 1) for start in starts], axis=1)


def pack(grid, clicks, mats, left):
    nx, ny, nz, rows, strip = grid.nx, grid.ny, grid.nz, grid.rows, grid.strip
    if grid.kernels:
        vmem, hbm = pl.BlockSpec(memory_space=pltpu.VMEM), pl.BlockSpec(memory_space=pltpu.HBM)
        tall = 2 * rows + CLICK_ROWS
        out = pl.pallas_call(
            functools.partial(pack_kernel, grid),
            out_shape=[jax.ShapeDtypeStruct((tall, grid.width), jnp.float32)] * (nx * ny)
            + [jax.ShapeDtypeStruct((strip, grid.cols), jnp.float32)],
            in_specs=[hbm] * 3,
            out_specs=[vmem] * (nx * ny + 1),
            scratch_shapes=[
                pltpu.VMEM(clicks.shape, jnp.int32),
                pltpu.SemaphoreType.DMA,
                pltpu.SemaphoreType.DMA((nx * ny, nz, 2)),
                pltpu.SemaphoreType.DMA((ny,)),
            ],
            compiler_params=pltpu.CompilerParams(vmem_limit_bytes=PACK_VMEM),
            cost_estimate=pl.CostEstimate(flops=0, bytes_accessed=2 * mats.size * 4, transcendentals=0),
        )(clicks, mats, left)
        return out[: nx * ny], out[nx * ny]
    _, x, y, _ = grid.here()
    pieces = []
    for dx in range(nx):
        for dy in range(ny):
            strips = []
            for zz in range(nz):
                start = zz * nx * rows + ((x + dx) % nx) * rows + ((y + dy) % ny) * strip
                strips.append(lax.dynamic_slice_in_dim(mats, start, strip, 2))
            pieces.append(jnp.concatenate(strips, axis=2).reshape(2 * rows, grid.width))
    return pieces, own_samples(grid, lax.dynamic_slice_in_dim(left, y * strip, strip, 0))


def collect_kernel(grid, sites, keys, *refs):
    pieces, (out_ref, held_ref, in_sems, out_sems) = dict(zip(keys, refs)), refs[-4:]
    _, _, y, core = grid.here()

    @pl.when(core == sites[0] % grid.cores)
    def _():
        for k, site in enumerate(sites):
            behind = lax.rem(y + grid.ny - site // grid.cores, grid.ny)
            for dx, dy in keys:

                @pl.when(behind == dy)
                def _():
                    pltpu.make_async_copy(pieces[dx, dy], held_ref.at[k, dx], in_sems.at[k, dx]).start()

        outward = []
        for k in range(len(sites)):
            for dx in range(grid.nx):
                pltpu.make_async_copy(refs[0], held_ref.at[k, dx], in_sems.at[k, dx]).wait()
                outward.append(pltpu.make_async_copy(held_ref.at[k, dx], out_ref.at[k, dx], out_sems.at[k, dx]))
                outward[-1].start()
        for copy in outward:
            copy.wait()


def collect(grid, sites, pieces, token=()):
    nx = grid.nx
    keys = tuple(pieces)
    tall, width = pieces[0, 0].shape
    if grid.kernels:
        hbm = pl.BlockSpec(memory_space=pl.ANY)
        shape = (len(sites), nx, tall, width)
        operands = list(pieces.values()) + list(token)
        return pl.pallas_call(
            functools.partial(collect_kernel, grid, tuple(sites), keys),
            out_shape=jax.ShapeDtypeStruct(shape, jnp.float32),
            in_specs=[hbm] * len(operands),
            out_specs=hbm,
            scratch_shapes=[
                pltpu.VMEM(shape, jnp.float32),
                pltpu.SemaphoreType.DMA(shape[:2]),
                pltpu.SemaphoreType.DMA(shape[:2]),
            ],
            compiler_params=pltpu.CompilerParams(vmem_limit_bytes=32 * 1024 * 1024),
            cost_estimate=pl.CostEstimate(flops=0, bytes_accessed=8 * len(sites) * nx * tall * width, transcendentals=0),
        )(*operands)
    mats = []
    for site in sites:
        behind = (grid.here()[2] - site // grid.cores) % grid.ny
        for dx in range(nx):
            value = pieces[dx, 0]
            for dy in range(1, grid.ny):
                value = jnp.where(behind == dy, pieces[dx, dy], value)
            mats.append(value)
    return jnp.stack(mats).reshape(len(sites), nx, tall, width)


def site_kernel(grid, site, last, tokens, *refs):
    nx, ny, nz, rows, strip, share = grid.nx, grid.ny, grid.nz, grid.rows, grid.strip, grid.share
    mats, refs = refs[: grid.cores], refs[grid.cores :]
    states, refs = refs[:nz], refs[nz + tokens :]
    outs = refs[: nx * ny]
    mat_ref, state_ref, high_ref, low_ref, sems, state_sems = refs[nx * ny :]
    z, _, y, core = grid.here()
    place = site // grid.cores
    inward = []
    for n, source in enumerate(grid.gathered_from(z)):
        at = pl.ds(pl.multiple_of(source * strip, strip), strip)
        inward.append(pltpu.make_async_copy(states[n], state_ref.at[at], state_sems.at[n]))
        inward[-1].start()

    for role, ref in enumerate(mats):

        @pl.when(core == role)
        def _():
            for dx in range(nx):
                pltpu.make_async_copy(ref.at[place, dx], mat_ref.at[dx], sems.at[dx]).start()

    for copy in inward:
        copy.wait()
    high_ref[...], low_ref[...] = halves(state_ref[...])
    for ex in range(nx):
        dx = (nx - ex) % nx
        pltpu.make_async_copy(mats[0].at[place, dx], mat_ref.at[dx], sems.at[dx]).wait()
        if ex == 0:
            clicks = mat_ref[0, 2 * rows : 2 * rows + CLICK_ROWS, :]
            row = lax.broadcasted_iota(jnp.int32, clicks.shape, 0)
            clicks = jnp.sum(jnp.where(row == core, clicks, 0.0), axis=0, keepdims=True)
        for ey in range(ny):
            to = lax.rem(y + ey, ny)
            out_ref = outs[ex * ny + ey]
            if last:
                columns = pl.ds(pl.multiple_of(to * share, share), share)
                b = (high_ref[:, columns], low_ref[:, columns])
                picked = jnp.zeros((1, share), jnp.float32)
                for yy in range(ny):
                    picked = jnp.where(to == yy, clicks[:, yy * share : (yy + 1) * share], picked)
                both = [dot3(halves(mat_ref[dx, o * rows : (o + 1) * rows, :]), b) for o in range(2)]
                out_ref[...] = jnp.where(picked == 1, both[1], both[0])
            else:
                at = pl.multiple_of(to * strip, strip)
                b = (high_ref[...], low_ref[...])
                both = [dot3(halves(mat_ref[dx, pl.ds(o * rows + at, strip), :]), b) for o in range(2)]
                out_ref[...] = jnp.where(clicks == 1, both[1], both[0])


def site_product(grid, site, clicks, mats, states, token=()):
    nx, ny, nz, rows, width, cols = grid.nx, grid.ny, grid.nz, grid.rows, grid.width, grid.cols
    last = site == grid.sites - 1
    shape = (rows, grid.share) if last else (grid.strip, cols)
    if grid.kernels:
        vmem, hbm = pl.BlockSpec(memory_space=pltpu.VMEM), pl.BlockSpec(memory_space=pl.ANY)
        tall = grid.rows * 2 + CLICK_ROWS
        flops = 2 * 3 * 2 * nx * rows * width * cols
        moved = 4 * (nx * tall * width + width * cols + nx * rows * cols)
        return pl.pallas_call(
            functools.partial(site_kernel, grid, site, last, len(token)),
            out_shape=[jax.ShapeDtypeStruct(shape, jnp.float32)] * (nx * ny),
            in_specs=[hbm] * (len(mats) + nz + len(token)),
            out_specs=[vmem] * (nx * ny),
            scratch_shapes=[
                pltpu.VMEM((nx, tall, width), jnp.float32),
                pltpu.VMEM((width, cols), jnp.float32),
                pltpu.VMEM((width, cols), jnp.bfloat16),
                pltpu.VMEM((width, cols), jnp.bfloat16),
                pltpu.SemaphoreType.DMA((nx,)),
                pltpu.SemaphoreType.DMA((nz,)),
            ],
            compiler_params=pltpu.CompilerParams(vmem_limit_bytes=32 * 1024 * 1024),
            cost_estimate=pl.CostEstimate(flops=flops, bytes_accessed=moved, transcendentals=0),
        )(*mats, *states, *token)
    z, _, y, core = grid.here()
    whole = jnp.zeros((width, cols), jnp.float32)
    for value, source in zip(states, grid.gathered_from(z)):
        whole = lax.dynamic_update_slice_in_dim(whole, value, source * grid.strip, 0)
    outs = []
    for ex in range(nx):
        dx = (nx - ex) % nx
        mat = 0
        for role, value in enumerate(mats):
            mat = jnp.where(core == role, value[site // grid.cores, dx], mat)
        both = jnp.dot(mat, whole, precision=lax.Precision.HIGH, preferred_element_type=jnp.float32)
        picked = jnp.where(clicks == 1, both[rows:], both[:rows])
        for ey in range(ny):
            axis = 1 if last else 0
            outs.append(lax.dynamic_slice_in_dim(picked, ((y + ey) % ny) * shape[axis], shape[axis], axis))
    return outs


def local(left_start, site_mats, clicks):
    sites, bonds = lax.axis_size("site"), lax.axis_size("bond")
    grid = Grid(sites, bonds, site_mats.shape[2], left_start.shape[1])
    nx, ny, nz, cores = grid.nx, grid.ny, grid.nz, grid.cores
    _, _, y, core = grid.here()
    pieces, state = pack(grid, clicks, site_mats[0], left_start)
    shifts = [(dx, dy) for dx in range(nx) for dy in range(ny)]

    own_clicks = {}
    if not grid.kernels:
        for dy in range(ny):
            for dcore in range(cores):
                own_clicks[dy, dcore] = grid.send(clicks, dy=dy, dcore=dcore) if dy or dcore else clicks

    def clicks_of(site):
        value = clicks
        for (dy, dcore), got in own_clicks.items():
            hit = ((y - site // cores) % ny == dy) & ((core - site % cores) % cores == dcore)
            value = jnp.where(hit, got, value)
        return own_samples(grid, value)

    def spread(which, pieces):
        got = {(dx, dy): grid.send(pieces[dx * ny + dy], dx=dx, dy=dy, cores=[which]) for dx, dy in shifts[:0:-1]}
        return {(0, 0): pieces[0], **got}

    mats = []
    for site in range(sites):
        gathered = grid.gather(state, relay=RELAY[min(site, 3)])
        token = []
        if site == 0:
            for which in range(cores):
                if which:
                    gathered[-1], later = lax.optimization_barrier((gathered[-1], pieces))
                mine = collect(grid, range(which, sites, cores), spread(which, later if which else pieces), gathered)
                others = [grid.send(mine, dcore=d, cores=[which]) for d in range(1, cores)]
                mats.append([([mine] + others)[(role - which) % cores] for role in range(cores)])
                token += [mine] if which else []
        outs = site_product(grid, site, clicks_of(site), mats[site % cores], gathered, token)
        state = outs[0]
        for ex, ey in shifts[:0:-1]:
            state = state + grid.send(outs[ex * ny + ey], dx=ex, dy=ey)
    return state


def solution(mesh):
    return jax.shard_map(
        local,
        mesh=mesh,
        in_specs=(P("bond", None), P("site", None, "bond", None), P("site", None)),
        out_specs=P("bond", "site"),
        check_vma=False,
    )
```

```python
import functools

import jax
import jax.numpy as jnp
from jax import lax
from jax.experimental import pallas as pl
from jax.experimental.pallas import tpu as pltpu
from jax.sharding import PartitionSpec as P


CLICK_ROWS = 8
PACK_VMEM = 48 * 1024 * 1024
RELAY = (True, True, False, True)


class Grid:
    def __init__(self, sites, bonds, rows, samples):
        self.sites, self.bonds = sites, bonds
        self.cores = 2 if sites % 2 == 0 else 1
        self.ny = sites // self.cores
        self.nx = max(q for q in range(1, bonds + 1) if bonds % q == 0 and q * q <= bonds)
        self.nz = bonds // self.nx
        self.rows = rows
        self.strip = rows // self.ny
        self.width = self.strip * self.nz
        self.share = samples // sites
        self.cols = self.share * self.ny
        aligned = self.strip % 128 == 0 and self.share % 128 == 0
        self.kernels = aligned and self.cols == self.width and self.cores <= CLICK_ROWS

    def here(self):
        site, bond = lax.axis_index("site"), lax.axis_index("bond")
        return bond // self.nx, bond % self.nx, site // self.cores, site % self.cores

    def index(self, z, x, y, core):
        site = (y % self.ny) * self.cores + core % self.cores
        return site * self.bonds + (z % self.nz) * self.nx + x % self.nx

    def send(self, value, dz=0, dx=0, dy=0, dcore=0, across=0, cores=None):
        pairs = []
        for z in range(self.nz):
            for x in range(self.nx):
                for y in range(self.ny):
                    for core in range(self.cores) if cores is None else cores:
                        to = self.index((z ^ across) + dz, x + dx, y + dy, core + dcore)
                        pairs.append((self.index(z, x, y, core), to))
        return lax.ppermute(value, ("site", "bond"), pairs)

    def gather(self, state, relay=False):
        if self.nz & (self.nz - 1):
            return [state] + [self.send(state, dz=self.nz - d) for d in range(1, self.nz)]
        got = [state]
        for d in range(1, self.nz):
            got.append(self.send(got[d ^ 1], across=1) if relay and d & 1 else self.send(state, across=d))
        return got

    def gathered_from(self, z):
        if self.nz & (self.nz - 1):
            return [lax.rem(z + d, self.nz) for d in range(self.nz)]
        return [z ^ d for d in range(self.nz)]


def halves(value):
    high = value.astype(jnp.bfloat16)
    low = (value - high.astype(jnp.float32)).astype(jnp.bfloat16)
    return high, low


def dot3(a, b):
    dot = functools.partial(jnp.dot, preferred_element_type=jnp.float32)
    return dot(a[0], b[0]) + (dot(a[0], b[1]) + dot(a[1], b[0]))


def pack_kernel(grid, clicks_ref, mats_ref, left_ref, *refs):
    nx, ny, nz, cores, rows, strip, share = grid.nx, grid.ny, grid.nz, grid.cores, grid.rows, grid.strip, grid.share
    piece_refs, state_ref = refs[: nx * ny], refs[nx * ny]
    clicks_held_ref, clicks_sem, in_sems, left_sems = refs[nx * ny + 1 :]
    _, x, y, core = grid.here()
    clicks_copy = pltpu.make_async_copy(clicks_ref, clicks_held_ref, clicks_sem)
    clicks_copy.start()
    order = [(dx, dy) for dx in reversed(range(nx)) for dy in reversed(range(ny))]
    into = {}
    for dx, dy in order:
        e = dx * ny + dy
        into[e] = []
        for zz in range(nz):
            start = zz * nx * rows + lax.rem(x + dx, nx) * rows + lax.rem(y + dy, ny) * strip
            columns = pl.ds(pl.multiple_of(start, strip), strip)
            for o in range(2):
                target = piece_refs[e].at[pl.ds(o * rows, rows), pl.ds(zz * strip, strip)]
                into[e].append(pltpu.make_async_copy(mats_ref.at[o, :, columns], target, in_sems.at[e, zz, o]))
        for copy in into[e]:
            copy.start()
    states = []
    for yy in range(ny):
        start = pl.multiple_of((yy * cores + core) * share, share)
        source = left_ref.at[pl.ds(pl.multiple_of(y * strip, strip), strip), pl.ds(start, share)]
        states.append(pltpu.make_async_copy(source, state_ref.at[:, pl.ds(yy * share, share)], left_sems.at[yy]))
    for copy in states:
        copy.start()
    clicks_copy.wait()
    for piece_ref in piece_refs:
        piece_ref[2 * rows :, :] = jnp.zeros((CLICK_ROWS, grid.width), jnp.float32)
        for c in range(cores):
            for yy in range(ny):
                start = (yy * cores + c) * share
                value = clicks_held_ref[:, start : start + share].astype(jnp.float32)
                piece_ref[2 * rows + c : 2 * rows + c + 1, yy * share : (yy + 1) * share] = value
    for copy in sum(into.values(), states):
        copy.wait()


def own_samples(grid, value):
    core = grid.here()[3]
    starts = [(yy * grid.cores + core) * grid.share for yy in range(grid.ny)]
    return jnp.concatenate([lax.dynamic_slice_in_dim(value, start, grid.share, 1) for start in starts], axis=1)


def pack(grid, clicks, mats, left):
    nx, ny, nz, rows, strip = grid.nx, grid.ny, grid.nz, grid.rows, grid.strip
    if grid.kernels:
        vmem, hbm = pl.BlockSpec(memory_space=pltpu.VMEM), pl.BlockSpec(memory_space=pltpu.HBM)
        tall = 2 * rows + CLICK_ROWS
        out = pl.pallas_call(
            functools.partial(pack_kernel, grid),
            out_shape=[jax.ShapeDtypeStruct((tall, grid.width), jnp.float32)] * (nx * ny)
            + [jax.ShapeDtypeStruct((strip, grid.cols), jnp.float32)],
            in_specs=[hbm] * 3,
            out_specs=[vmem] * (nx * ny + 1),
            scratch_shapes=[
                pltpu.VMEM(clicks.shape, jnp.int32),
                pltpu.SemaphoreType.DMA,
                pltpu.SemaphoreType.DMA((nx * ny, nz, 2)),
                pltpu.SemaphoreType.DMA((ny,)),
            ],
            compiler_params=pltpu.CompilerParams(vmem_limit_bytes=PACK_VMEM),
            cost_estimate=pl.CostEstimate(flops=0, bytes_accessed=2 * mats.size * 4, transcendentals=0),
        )(clicks, mats, left)
        return out[: nx * ny], out[nx * ny]
    _, x, y, _ = grid.here()
    pieces = []
    for dx in range(nx):
        for dy in range(ny):
            strips = []
            for zz in range(nz):
                start = zz * nx * rows + ((x + dx) % nx) * rows + ((y + dy) % ny) * strip
                strips.append(lax.dynamic_slice_in_dim(mats, start, strip, 2))
            pieces.append(jnp.concatenate(strips, axis=2).reshape(2 * rows, grid.width))
    return pieces, own_samples(grid, lax.dynamic_slice_in_dim(left, y * strip, strip, 0))


def collect_kernel(grid, sites, keys, *refs):
    pieces, (out_ref, held_ref, in_sems, out_sems) = dict(zip(keys, refs)), refs[-4:]
    _, _, y, core = grid.here()

    @pl.when(core == sites[0] % grid.cores)
    def _():
        for k, site in enumerate(sites):
            behind = lax.rem(y + grid.ny - site // grid.cores, grid.ny)
            for dx, dy in keys:

                @pl.when(behind == dy)
                def _():
                    pltpu.make_async_copy(pieces[dx, dy], held_ref.at[k, dx], in_sems.at[k, dx]).start()

        outward = []
        for k in range(len(sites)):
            for dx in range(grid.nx):
                pltpu.make_async_copy(refs[0], held_ref.at[k, dx], in_sems.at[k, dx]).wait()
                outward.append(pltpu.make_async_copy(held_ref.at[k, dx], out_ref.at[k, dx], out_sems.at[k, dx]))
                outward[-1].start()
        for copy in outward:
            copy.wait()


def collect(grid, sites, pieces, token=()):
    nx = grid.nx
    keys = tuple(pieces)
    tall, width = pieces[0, 0].shape
    if grid.kernels:
        hbm = pl.BlockSpec(memory_space=pl.ANY)
        shape = (len(sites), nx, tall, width)
        operands = list(pieces.values()) + list(token)
        return pl.pallas_call(
            functools.partial(collect_kernel, grid, tuple(sites), keys),
            out_shape=jax.ShapeDtypeStruct(shape, jnp.float32),
            in_specs=[hbm] * len(operands),
            out_specs=hbm,
            scratch_shapes=[
                pltpu.VMEM(shape, jnp.float32),
                pltpu.SemaphoreType.DMA(shape[:2]),
                pltpu.SemaphoreType.DMA(shape[:2]),
            ],
            compiler_params=pltpu.CompilerParams(vmem_limit_bytes=32 * 1024 * 1024),
            cost_estimate=pl.CostEstimate(flops=0, bytes_accessed=8 * len(sites) * nx * tall * width, transcendentals=0),
        )(*operands)
    mats = []
    for site in sites:
        behind = (grid.here()[2] - site // grid.cores) % grid.ny
        for dx in range(nx):
            value = pieces[dx, 0]
            for dy in range(1, grid.ny):
                value = jnp.where(behind == dy, pieces[dx, dy], value)
            mats.append(value)
    return jnp.stack(mats).reshape(len(sites), nx, tall, width)


def site_kernel(grid, site, last, tokens, *refs):
    nx, ny, nz, rows, strip, share = grid.nx, grid.ny, grid.nz, grid.rows, grid.strip, grid.share
    mats, refs = refs[: grid.cores], refs[grid.cores :]
    states, refs = refs[:nz], refs[nz + tokens :]
    outs = refs[: nx * ny]
    mat_ref, state_ref, high_ref, low_ref, sems, state_sems = refs[nx * ny :]
    z, _, y, core = grid.here()
    place = site // grid.cores
    inward = []
    for n, source in enumerate(grid.gathered_from(z)):
        at = pl.ds(pl.multiple_of(source * strip, strip), strip)
        inward.append(pltpu.make_async_copy(states[n], state_ref.at[at], state_sems.at[n]))
        inward[-1].start()

    for role, ref in enumerate(mats):

        @pl.when(core == role)
        def _():
            for dx in range(nx):
                pltpu.make_async_copy(ref.at[place, dx], mat_ref.at[dx], sems.at[dx]).start()

    for copy in inward:
        copy.wait()
    high_ref[...], low_ref[...] = halves(state_ref[...])
    for ex in range(nx):
        dx = (nx - ex) % nx
        pltpu.make_async_copy(mats[0].at[place, dx], mat_ref.at[dx], sems.at[dx]).wait()
        if ex == 0:
            clicks = mat_ref[0, 2 * rows : 2 * rows + CLICK_ROWS, :]
            row = lax.broadcasted_iota(jnp.int32, clicks.shape, 0)
            clicks = jnp.sum(jnp.where(row == core, clicks, 0.0), axis=0, keepdims=True)
        for ey in range(ny):
            to = lax.rem(y + ey, ny)
            out_ref = outs[ex * ny + ey]
            if last:
                columns = pl.ds(pl.multiple_of(to * share, share), share)
                b = (high_ref[:, columns], low_ref[:, columns])
                picked = jnp.zeros((1, share), jnp.float32)
                for yy in range(ny):
                    picked = jnp.where(to == yy, clicks[:, yy * share : (yy + 1) * share], picked)
                both = [dot3(halves(mat_ref[dx, o * rows : (o + 1) * rows, :]), b) for o in range(2)]
                out_ref[...] = jnp.where(picked == 1, both[1], both[0])
            else:
                at = pl.multiple_of(to * strip, strip)
                b = (high_ref[...], low_ref[...])
                both = [dot3(halves(mat_ref[dx, pl.ds(o * rows + at, strip), :]), b) for o in range(2)]
                out_ref[...] = jnp.where(clicks == 1, both[1], both[0])


def site_product(grid, site, clicks, mats, states, token=()):
    nx, ny, nz, rows, width, cols = grid.nx, grid.ny, grid.nz, grid.rows, grid.width, grid.cols
    last = site == grid.sites - 1
    shape = (rows, grid.share) if last else (grid.strip, cols)
    if grid.kernels:
        vmem, hbm = pl.BlockSpec(memory_space=pltpu.VMEM), pl.BlockSpec(memory_space=pl.ANY)
        tall = grid.rows * 2 + CLICK_ROWS
        flops = 2 * 3 * 2 * nx * rows * width * cols
        moved = 4 * (nx * tall * width + width * cols + nx * rows * cols)
        return pl.pallas_call(
            functools.partial(site_kernel, grid, site, last, len(token)),
            out_shape=[jax.ShapeDtypeStruct(shape, jnp.float32)] * (nx * ny),
            in_specs=[hbm] * (len(mats) + nz + len(token)),
            out_specs=[vmem] * (nx * ny),
            scratch_shapes=[
                pltpu.VMEM((nx, tall, width), jnp.float32),
                pltpu.VMEM((width, cols), jnp.float32),
                pltpu.VMEM((width, cols), jnp.bfloat16),
                pltpu.VMEM((width, cols), jnp.bfloat16),
                pltpu.SemaphoreType.DMA((nx,)),
                pltpu.SemaphoreType.DMA((nz,)),
            ],
            compiler_params=pltpu.CompilerParams(vmem_limit_bytes=32 * 1024 * 1024),
            cost_estimate=pl.CostEstimate(flops=flops, bytes_accessed=moved, transcendentals=0),
        )(*mats, *states, *token)
    z, _, y, core = grid.here()
    whole = jnp.zeros((width, cols), jnp.float32)
    for value, source in zip(states, grid.gathered_from(z)):
        whole = lax.dynamic_update_slice_in_dim(whole, value, source * grid.strip, 0)
    outs = []
    for ex in range(nx):
        dx = (nx - ex) % nx
        mat = 0
        for role, value in enumerate(mats):
            mat = jnp.where(core == role, value[site // grid.cores, dx], mat)
        both = jnp.dot(mat, whole, precision=lax.Precision.HIGH, preferred_element_type=jnp.float32)
        picked = jnp.where(clicks == 1, both[rows:], both[:rows])
        for ey in range(ny):
            axis = 1 if last else 0
            outs.append(lax.dynamic_slice_in_dim(picked, ((y + ey) % ny) * shape[axis], shape[axis], axis))
    return outs


def local(left_start, site_mats, clicks):
    sites, bonds = lax.axis_size("site"), lax.axis_size("bond")
    grid = Grid(sites, bonds, site_mats.shape[2], left_start.shape[1])
    nx, ny, nz, cores = grid.nx, grid.ny, grid.nz, grid.cores
    _, _, y, core = grid.here()
    pieces, state = pack(grid, clicks, site_mats[0], left_start)
    shifts = [(dx, dy) for dx in range(nx) for dy in range(ny)]

    own_clicks = {}
    if not grid.kernels:
        for dy in range(ny):
            for dcore in range(cores):
                own_clicks[dy, dcore] = grid.send(clicks, dy=dy, dcore=dcore) if dy or dcore else clicks

    def clicks_of(site):
        value = clicks
        for (dy, dcore), got in own_clicks.items():
            hit = ((y - site // cores) % ny == dy) & ((core - site % cores) % cores == dcore)
            value = jnp.where(hit, got, value)
        return own_samples(grid, value)

    def spread(which, pieces):
        got, own = {}, pieces[0]
        for dx, dy in shifts[:0:-1]:
            if which and not (dx and dy) and (nx - 1, ny - 1) in got:
                got[nx - 1, ny - 1], pieces = lax.optimization_barrier((got[nx - 1, ny - 1], pieces))
            got[dx, dy] = grid.send(pieces[dx * ny + dy], dx=dx, dy=dy, cores=[which])
        return {(0, 0): own, **got}

    mats = []
    for site in range(sites):
        gathered = grid.gather(state, relay=RELAY[min(site, 3)])
        token = []
        if site == 0:
            after, later = [], pieces
            for which in range(cores):
                if which:
                    gathered, after, later = lax.optimization_barrier((gathered, list(got.values())[1:], pieces))
                got = spread(which, later)
                mine = collect(grid, range(which, sites, cores), got, gathered + after)
                others = [grid.send(mine, dcore=d, cores=[which]) for d in range(1, cores)]
                mats.append([([mine] + others)[(role - which) % cores] for role in range(cores)])
                token += [mine] if which else []
        outs = site_product(grid, site, clicks_of(site), mats[site % cores], gathered, token)
        state = outs[0]
        for ex, ey in shifts[:0:-1]:
            state = state + grid.send(outs[ex * ny + ey], dx=ex, dy=ey)
    return state


def solution(mesh):
    return jax.shard_map(
        local,
        mesh=mesh,
        in_specs=(P("bond", None), P("site", None, "bond", None), P("site", None)),
        out_specs=P("bond", "site"),
        check_vma=False,
    )
```

```python
import functools

import jax
import jax.numpy as jnp
from jax import lax
from jax.experimental import pallas as pl
from jax.experimental.pallas import tpu as pltpu
from jax.sharding import PartitionSpec as P


CLICK_ROWS = 8
PACK_VMEM = 48 * 1024 * 1024
RELAY = (True, True, False, False)


class Grid:
    def __init__(self, sites, bonds, rows, samples):
        self.sites, self.bonds = sites, bonds
        self.cores = 2 if sites % 2 == 0 else 1
        self.ny = sites // self.cores
        self.nx = max(q for q in range(1, bonds + 1) if bonds % q == 0 and q * q <= bonds)
        self.nz = bonds // self.nx
        self.rows = rows
        self.strip = rows // self.ny
        self.width = self.strip * self.nz
        self.share = samples // sites
        self.cols = self.share * self.ny
        aligned = self.strip % 128 == 0 and self.share % 128 == 0
        self.kernels = aligned and self.cols == self.width and self.cores <= CLICK_ROWS

    def here(self):
        site, bond = lax.axis_index("site"), lax.axis_index("bond")
        return bond // self.nx, bond % self.nx, site // self.cores, site % self.cores

    def index(self, z, x, y, core):
        site = (y % self.ny) * self.cores + core % self.cores
        return site * self.bonds + (z % self.nz) * self.nx + x % self.nx

    def send(self, value, dz=0, dx=0, dy=0, dcore=0, across=0, cores=None):
        pairs = []
        for z in range(self.nz):
            for x in range(self.nx):
                for y in range(self.ny):
                    for core in range(self.cores) if cores is None else cores:
                        to = self.index((z ^ across) + dz, x + dx, y + dy, core + dcore)
                        pairs.append((self.index(z, x, y, core), to))
        return lax.ppermute(value, ("site", "bond"), pairs)

    def gather(self, state, relay=False):
        if self.nz & (self.nz - 1):
            return [state] + [self.send(state, dz=self.nz - d) for d in range(1, self.nz)]
        got = [state]
        for d in range(1, self.nz):
            got.append(self.send(got[d ^ 1], across=1) if relay and d & 1 else self.send(state, across=d))
        return got

    def gathered_from(self, z):
        if self.nz & (self.nz - 1):
            return [lax.rem(z + d, self.nz) for d in range(self.nz)]
        return [z ^ d for d in range(self.nz)]


def halves(value):
    high = value.astype(jnp.bfloat16)
    low = (value - high.astype(jnp.float32)).astype(jnp.bfloat16)
    return high, low


def dot3(a, b):
    dot = functools.partial(jnp.dot, preferred_element_type=jnp.float32)
    return dot(a[0], b[0]) + (dot(a[0], b[1]) + dot(a[1], b[0]))


def pack_kernel(grid, clicks_ref, mats_ref, left_ref, *refs):
    nx, ny, nz, cores, rows, strip, share = grid.nx, grid.ny, grid.nz, grid.cores, grid.rows, grid.strip, grid.share
    piece_refs, state_ref = refs[: nx * ny], refs[nx * ny]
    clicks_held_ref, clicks_sem, in_sems, left_sems = refs[nx * ny + 1 :]
    _, x, y, core = grid.here()
    clicks_copy = pltpu.make_async_copy(clicks_ref, clicks_held_ref, clicks_sem)
    clicks_copy.start()
    order = [(dx, dy) for dx in reversed(range(nx)) for dy in reversed(range(ny))]
    into = {}
    for dx, dy in order:
        e = dx * ny + dy
        into[e] = []
        for zz in range(nz):
            start = zz * nx * rows + lax.rem(x + dx, nx) * rows + lax.rem(y + dy, ny) * strip
            columns = pl.ds(pl.multiple_of(start, strip), strip)
            for o in range(2):
                target = piece_refs[e].at[pl.ds(o * rows, rows), pl.ds(zz * strip, strip)]
                into[e].append(pltpu.make_async_copy(mats_ref.at[o, :, columns], target, in_sems.at[e, zz, o]))
        for copy in into[e]:
            copy.start()
    states = []
    for yy in range(ny):
        start = pl.multiple_of((yy * cores + core) * share, share)
        source = left_ref.at[pl.ds(pl.multiple_of(y * strip, strip), strip), pl.ds(start, share)]
        states.append(pltpu.make_async_copy(source, state_ref.at[:, pl.ds(yy * share, share)], left_sems.at[yy]))
    for copy in states:
        copy.start()
    clicks_copy.wait()
    for piece_ref in piece_refs:
        piece_ref[2 * rows :, :] = jnp.zeros((CLICK_ROWS, grid.width), jnp.float32)
        for c in range(cores):
            for yy in range(ny):
                start = (yy * cores + c) * share
                value = clicks_held_ref[:, start : start + share].astype(jnp.float32)
                piece_ref[2 * rows + c : 2 * rows + c + 1, yy * share : (yy + 1) * share] = value
    for copy in sum(into.values(), states):
        copy.wait()


def own_samples(grid, value):
    core = grid.here()[3]
    starts = [(yy * grid.cores + core) * grid.share for yy in range(grid.ny)]
    return jnp.concatenate([lax.dynamic_slice_in_dim(value, start, grid.share, 1) for start in starts], axis=1)


def pack(grid, clicks, mats, left):
    nx, ny, nz, rows, strip = grid.nx, grid.ny, grid.nz, grid.rows, grid.strip
    if grid.kernels:
        vmem, hbm = pl.BlockSpec(memory_space=pltpu.VMEM), pl.BlockSpec(memory_space=pltpu.HBM)
        tall = 2 * rows + CLICK_ROWS
        out = pl.pallas_call(
            functools.partial(pack_kernel, grid),
            out_shape=[jax.ShapeDtypeStruct((tall, grid.width), jnp.float32)] * (nx * ny)
            + [jax.ShapeDtypeStruct((strip, grid.cols), jnp.float32)],
            in_specs=[hbm] * 3,
            out_specs=[vmem] * (nx * ny + 1),
            scratch_shapes=[
                pltpu.VMEM(clicks.shape, jnp.int32),
                pltpu.SemaphoreType.DMA,
                pltpu.SemaphoreType.DMA((nx * ny, nz, 2)),
                pltpu.SemaphoreType.DMA((ny,)),
            ],
            compiler_params=pltpu.CompilerParams(vmem_limit_bytes=PACK_VMEM),
            cost_estimate=pl.CostEstimate(flops=0, bytes_accessed=2 * mats.size * 4, transcendentals=0),
        )(clicks, mats, left)
        return out[: nx * ny], out[nx * ny]
    _, x, y, _ = grid.here()
    pieces = []
    for dx in range(nx):
        for dy in range(ny):
            strips = []
            for zz in range(nz):
                start = zz * nx * rows + ((x + dx) % nx) * rows + ((y + dy) % ny) * strip
                strips.append(lax.dynamic_slice_in_dim(mats, start, strip, 2))
            pieces.append(jnp.concatenate(strips, axis=2).reshape(2 * rows, grid.width))
    return pieces, own_samples(grid, lax.dynamic_slice_in_dim(left, y * strip, strip, 0))


def collect_kernel(grid, sites, keys, *refs):
    pieces, (out_ref, held_ref, in_sems, out_sems) = dict(zip(keys, refs)), refs[-4:]
    _, _, y, core = grid.here()

    @pl.when(core == sites[0] % grid.cores)
    def _():
        for k, site in enumerate(sites):
            behind = lax.rem(y + grid.ny - site // grid.cores, grid.ny)
            for dx, dy in keys:

                @pl.when(behind == dy)
                def _():
                    pltpu.make_async_copy(pieces[dx, dy], held_ref.at[k, dx], in_sems.at[k, dx]).start()

        outward = []
        for k in range(len(sites)):
            for dx in range(grid.nx):
                pltpu.make_async_copy(refs[0], held_ref.at[k, dx], in_sems.at[k, dx]).wait()
                outward.append(pltpu.make_async_copy(held_ref.at[k, dx], out_ref.at[k, dx], out_sems.at[k, dx]))
                outward[-1].start()
        for copy in outward:
            copy.wait()


def collect(grid, sites, pieces, token=()):
    nx = grid.nx
    keys = tuple(pieces)
    tall, width = pieces[0, 0].shape
    if grid.kernels:
        hbm = pl.BlockSpec(memory_space=pl.ANY)
        shape = (len(sites), nx, tall, width)
        operands = list(pieces.values()) + list(token)
        return pl.pallas_call(
            functools.partial(collect_kernel, grid, tuple(sites), keys),
            out_shape=jax.ShapeDtypeStruct(shape, jnp.float32),
            in_specs=[hbm] * len(operands),
            out_specs=hbm,
            scratch_shapes=[
                pltpu.VMEM(shape, jnp.float32),
                pltpu.SemaphoreType.DMA(shape[:2]),
                pltpu.SemaphoreType.DMA(shape[:2]),
            ],
            compiler_params=pltpu.CompilerParams(vmem_limit_bytes=32 * 1024 * 1024),
            cost_estimate=pl.CostEstimate(flops=0, bytes_accessed=8 * len(sites) * nx * tall * width, transcendentals=0),
        )(*operands)
    mats = []
    for site in sites:
        behind = (grid.here()[2] - site // grid.cores) % grid.ny
        for dx in range(nx):
            value = pieces[dx, 0]
            for dy in range(1, grid.ny):
                value = jnp.where(behind == dy, pieces[dx, dy], value)
            mats.append(value)
    return jnp.stack(mats).reshape(len(sites), nx, tall, width)


def site_kernel(grid, site, last, tokens, *refs):
    nx, ny, nz, rows, strip, share = grid.nx, grid.ny, grid.nz, grid.rows, grid.strip, grid.share
    mats, refs = refs[: grid.cores], refs[grid.cores :]
    states, refs = refs[:nz], refs[nz + tokens :]
    outs = refs[: nx * ny]
    mat_ref, state_ref, high_ref, low_ref, sems, state_sems = refs[nx * ny :]
    z, _, y, core = grid.here()
    place = site // grid.cores
    inward = []
    for n, source in enumerate(grid.gathered_from(z)):
        at = pl.ds(pl.multiple_of(source * strip, strip), strip)
        inward.append(pltpu.make_async_copy(states[n], state_ref.at[at], state_sems.at[n]))
        inward[-1].start()

    for role, ref in enumerate(mats):

        @pl.when(core == role)
        def _():
            for dx in range(nx):
                pltpu.make_async_copy(ref.at[place, dx], mat_ref.at[dx], sems.at[dx]).start()

    for copy in inward:
        copy.wait()
    high_ref[...], low_ref[...] = halves(state_ref[...])
    for ex in range(nx):
        dx = (nx - ex) % nx
        pltpu.make_async_copy(mats[0].at[place, dx], mat_ref.at[dx], sems.at[dx]).wait()
        if ex == 0:
            clicks = mat_ref[0, 2 * rows : 2 * rows + CLICK_ROWS, :]
            row = lax.broadcasted_iota(jnp.int32, clicks.shape, 0)
            clicks = jnp.sum(jnp.where(row == core, clicks, 0.0), axis=0, keepdims=True)
        for ey in range(ny):
            to = lax.rem(y + ey, ny)
            out_ref = outs[ex * ny + ey]
            if last:
                columns = pl.ds(pl.multiple_of(to * share, share), share)
                b = (high_ref[:, columns], low_ref[:, columns])
                picked = jnp.zeros((1, share), jnp.float32)
                for yy in range(ny):
                    picked = jnp.where(to == yy, clicks[:, yy * share : (yy + 1) * share], picked)
                both = [dot3(halves(mat_ref[dx, o * rows : (o + 1) * rows, :]), b) for o in range(2)]
                out_ref[...] = jnp.where(picked == 1, both[1], both[0])
            else:
                at = pl.multiple_of(to * strip, strip)
                b = (high_ref[...], low_ref[...])
                both = [dot3(halves(mat_ref[dx, pl.ds(o * rows + at, strip), :]), b) for o in range(2)]
                out_ref[...] = jnp.where(clicks == 1, both[1], both[0])


def site_product(grid, site, clicks, mats, states, token=()):
    nx, ny, nz, rows, width, cols = grid.nx, grid.ny, grid.nz, grid.rows, grid.width, grid.cols
    last = site == grid.sites - 1
    shape = (rows, grid.share) if last else (grid.strip, cols)
    if grid.kernels:
        vmem, hbm = pl.BlockSpec(memory_space=pltpu.VMEM), pl.BlockSpec(memory_space=pl.ANY)
        tall = grid.rows * 2 + CLICK_ROWS
        flops = 2 * 3 * 2 * nx * rows * width * cols
        moved = 4 * (nx * tall * width + width * cols + nx * rows * cols)
        return pl.pallas_call(
            functools.partial(site_kernel, grid, site, last, len(token)),
            out_shape=[jax.ShapeDtypeStruct(shape, jnp.float32)] * (nx * ny),
            in_specs=[hbm] * (len(mats) + nz + len(token)),
            out_specs=[vmem] * (nx * ny),
            scratch_shapes=[
                pltpu.VMEM((nx, tall, width), jnp.float32),
                pltpu.VMEM((width, cols), jnp.float32),
                pltpu.VMEM((width, cols), jnp.bfloat16),
                pltpu.VMEM((width, cols), jnp.bfloat16),
                pltpu.SemaphoreType.DMA((nx,)),
                pltpu.SemaphoreType.DMA((nz,)),
            ],
            compiler_params=pltpu.CompilerParams(vmem_limit_bytes=32 * 1024 * 1024),
            cost_estimate=pl.CostEstimate(flops=flops, bytes_accessed=moved, transcendentals=0),
        )(*mats, *states, *token)
    z, _, y, core = grid.here()
    whole = jnp.zeros((width, cols), jnp.float32)
    for value, source in zip(states, grid.gathered_from(z)):
        whole = lax.dynamic_update_slice_in_dim(whole, value, source * grid.strip, 0)
    outs = []
    for ex in range(nx):
        dx = (nx - ex) % nx
        mat = 0
        for role, value in enumerate(mats):
            mat = jnp.where(core == role, value[site // grid.cores, dx], mat)
        both = jnp.dot(mat, whole, precision=lax.Precision.HIGH, preferred_element_type=jnp.float32)
        picked = jnp.where(clicks == 1, both[rows:], both[:rows])
        for ey in range(ny):
            axis = 1 if last else 0
            outs.append(lax.dynamic_slice_in_dim(picked, ((y + ey) % ny) * shape[axis], shape[axis], axis))
    return outs


def local(left_start, site_mats, clicks):
    sites, bonds = lax.axis_size("site"), lax.axis_size("bond")
    grid = Grid(sites, bonds, site_mats.shape[2], left_start.shape[1])
    nx, ny, nz, cores = grid.nx, grid.ny, grid.nz, grid.cores
    _, _, y, core = grid.here()
    pieces, state = pack(grid, clicks, site_mats[0], left_start)
    shifts = [(dx, dy) for dx in range(nx) for dy in range(ny)]

    own_clicks = {}
    if not grid.kernels:
        for dy in range(ny):
            for dcore in range(cores):
                own_clicks[dy, dcore] = grid.send(clicks, dy=dy, dcore=dcore) if dy or dcore else clicks

    def clicks_of(site):
        value = clicks
        for (dy, dcore), got in own_clicks.items():
            hit = ((y - site // cores) % ny == dy) & ((core - site % cores) % cores == dcore)
            value = jnp.where(hit, got, value)
        return own_samples(grid, value)

    def spread(which, pieces):
        got, own = {}, pieces[0]
        for dx, dy in shifts[:0:-1]:
            if which and not (dx and dy) and (nx - 1, ny - 1) in got:
                got[nx - 1, ny - 1], pieces = lax.optimization_barrier((got[nx - 1, ny - 1], pieces))
            got[dx, dy] = grid.send(pieces[dx * ny + dy], dx=dx, dy=dy, cores=[which])
        return {(0, 0): own, **got}

    def across(mine, which):
        others = [grid.send(mine, dcore=d, cores=[which]) for d in range(1, cores)]
        return [([mine] + others)[(role - which) % cores] for role in range(cores)]

    mats = []
    for site in range(sites):
        gathered = grid.gather(state, relay=RELAY[min(site, 3)])
        token = []
        if site == 0:
            got = spread(0, pieces)
            mats.append(across(collect(grid, range(0, sites, cores), got, gathered), 0))
            for which in range(1, cores):
                gathered, after, later = lax.optimization_barrier((gathered, list(got.values())[1:], pieces))
                got = spread(which, later)
                token += [got[0, 1]] + after
        outs = site_product(grid, site, clicks_of(site), mats[site % cores], gathered, token)
        if site == 0 and cores > 1:
            mats.append(across(collect(grid, range(1, sites, cores), got, outs[:1]), 1))
        state = outs[0]
        for ex, ey in shifts[:0:-1]:
            state = state + grid.send(outs[ex * ny + ey], dx=ex, dy=ey)
    return state


def solution(mesh):
    return jax.shard_map(
        local,
        mesh=mesh,
        in_specs=(P("bond", None), P("site", None, "bond", None), P("site", None)),
        out_specs=P("bond", "site"),
        check_vma=False,
    )
```

```python
import functools

import jax
import jax.numpy as jnp
from jax import lax
from jax.experimental import pallas as pl
from jax.experimental.pallas import tpu as pltpu
from jax.sharding import PartitionSpec as P


CLICK_ROWS = 8
PACK_VMEM = 48 * 1024 * 1024
RELAY = (True, True, False, False)


class Grid:
    def __init__(self, sites, bonds, rows, samples):
        self.sites, self.bonds = sites, bonds
        self.cores = 2 if sites % 2 == 0 else 1
        self.ny = sites // self.cores
        self.nx = max(q for q in range(1, bonds + 1) if bonds % q == 0 and q * q <= bonds)
        self.nz = bonds // self.nx
        self.rows = rows
        self.strip = rows // self.ny
        self.width = self.strip * self.nz
        self.share = samples // sites
        self.cols = self.share * self.ny
        aligned = self.strip % 128 == 0 and self.share % 128 == 0
        self.kernels = aligned and self.cols == self.width and self.cores <= CLICK_ROWS

    def here(self):
        site, bond = lax.axis_index("site"), lax.axis_index("bond")
        return bond // self.nx, bond % self.nx, site // self.cores, site % self.cores

    def index(self, z, x, y, core):
        site = (y % self.ny) * self.cores + core % self.cores
        return site * self.bonds + (z % self.nz) * self.nx + x % self.nx

    def send(self, value, dz=0, dx=0, dy=0, dcore=0, across=0, cores=None):
        pairs = []
        for z in range(self.nz):
            for x in range(self.nx):
                for y in range(self.ny):
                    for core in range(self.cores) if cores is None else cores:
                        to = self.index((z ^ across) + dz, x + dx, y + dy, core + dcore)
                        pairs.append((self.index(z, x, y, core), to))
        return lax.ppermute(value, ("site", "bond"), pairs)

    def gather(self, state, relay=False):
        if self.nz & (self.nz - 1):
            return [state] + [self.send(state, dz=self.nz - d) for d in range(1, self.nz)]
        got = [state]
        for d in range(1, self.nz):
            got.append(self.send(got[d ^ 1], across=1) if relay and d & 1 else self.send(state, across=d))
        return got

    def gathered_from(self, z):
        if self.nz & (self.nz - 1):
            return [lax.rem(z + d, self.nz) for d in range(self.nz)]
        return [z ^ d for d in range(self.nz)]


def halves(value):
    high = value.astype(jnp.bfloat16)
    low = (value - high.astype(jnp.float32)).astype(jnp.bfloat16)
    return high, low


def dot3(a, b):
    dot = functools.partial(jnp.dot, preferred_element_type=jnp.float32)
    return dot(a[0], b[0]) + (dot(a[0], b[1]) + dot(a[1], b[0]))


def pack_kernel(grid, clicks_ref, mats_ref, left_ref, *refs):
    nx, ny, nz, cores, rows, strip, share = grid.nx, grid.ny, grid.nz, grid.cores, grid.rows, grid.strip, grid.share
    piece_refs, state_ref = refs[: nx * ny], refs[nx * ny]
    clicks_held_ref, clicks_sem, in_sems, left_sems = refs[nx * ny + 1 :]
    _, x, y, core = grid.here()
    clicks_copy = pltpu.make_async_copy(clicks_ref, clicks_held_ref, clicks_sem)
    clicks_copy.start()
    order = [(dx, dy) for dx in reversed(range(nx)) for dy in reversed(range(ny))]
    into = {}
    for dx, dy in order:
        e = dx * ny + dy
        into[e] = []
        for zz in range(nz):
            start = zz * nx * rows + lax.rem(x + dx, nx) * rows + lax.rem(y + dy, ny) * strip
            columns = pl.ds(pl.multiple_of(start, strip), strip)
            for o in range(2):
                target = piece_refs[e].at[pl.ds(o * rows, rows), pl.ds(zz * strip, strip)]
                into[e].append(pltpu.make_async_copy(mats_ref.at[o, :, columns], target, in_sems.at[e, zz, o]))
        for copy in into[e]:
            copy.start()
    states = []
    for yy in range(ny):
        start = pl.multiple_of((yy * cores + core) * share, share)
        source = left_ref.at[pl.ds(pl.multiple_of(y * strip, strip), strip), pl.ds(start, share)]
        states.append(pltpu.make_async_copy(source, state_ref.at[:, pl.ds(yy * share, share)], left_sems.at[yy]))
    for copy in states:
        copy.start()
    clicks_copy.wait()
    for piece_ref in piece_refs:
        piece_ref[2 * rows :, :] = jnp.zeros((CLICK_ROWS, grid.width), jnp.float32)
        for c in range(cores):
            for yy in range(ny):
                start = (yy * cores + c) * share
                value = clicks_held_ref[:, start : start + share].astype(jnp.float32)
                piece_ref[2 * rows + c : 2 * rows + c + 1, yy * share : (yy + 1) * share] = value
    for copy in sum(into.values(), states):
        copy.wait()


def own_samples(grid, value):
    core = grid.here()[3]
    starts = [(yy * grid.cores + core) * grid.share for yy in range(grid.ny)]
    return jnp.concatenate([lax.dynamic_slice_in_dim(value, start, grid.share, 1) for start in starts], axis=1)


def pack(grid, clicks, mats, left):
    nx, ny, nz, rows, strip = grid.nx, grid.ny, grid.nz, grid.rows, grid.strip
    if grid.kernels:
        vmem, hbm = pl.BlockSpec(memory_space=pltpu.VMEM), pl.BlockSpec(memory_space=pltpu.HBM)
        tall = 2 * rows + CLICK_ROWS
        out = pl.pallas_call(
            functools.partial(pack_kernel, grid),
            out_shape=[jax.ShapeDtypeStruct((tall, grid.width), jnp.float32)] * (nx * ny)
            + [jax.ShapeDtypeStruct((strip, grid.cols), jnp.float32)],
            in_specs=[hbm] * 3,
            out_specs=[vmem] * (nx * ny + 1),
            scratch_shapes=[
                pltpu.VMEM(clicks.shape, jnp.int32),
                pltpu.SemaphoreType.DMA,
                pltpu.SemaphoreType.DMA((nx * ny, nz, 2)),
                pltpu.SemaphoreType.DMA((ny,)),
            ],
            compiler_params=pltpu.CompilerParams(vmem_limit_bytes=PACK_VMEM),
            cost_estimate=pl.CostEstimate(flops=0, bytes_accessed=2 * mats.size * 4, transcendentals=0),
        )(clicks, mats, left)
        return out[: nx * ny], out[nx * ny]
    _, x, y, _ = grid.here()
    pieces = []
    for dx in range(nx):
        for dy in range(ny):
            strips = []
            for zz in range(nz):
                start = zz * nx * rows + ((x + dx) % nx) * rows + ((y + dy) % ny) * strip
                strips.append(lax.dynamic_slice_in_dim(mats, start, strip, 2))
            pieces.append(jnp.concatenate(strips, axis=2).reshape(2 * rows, grid.width))
    return pieces, own_samples(grid, lax.dynamic_slice_in_dim(left, y * strip, strip, 0))


def collect_kernel(grid, sites, keys, *refs):
    pieces, (out_ref, in_sems) = dict(zip(keys, refs)), refs[-2:]
    _, _, y, core = grid.here()

    @pl.when(core == sites[0] % grid.cores)
    def _():
        for k, site in enumerate(sites):
            behind = lax.rem(y + grid.ny - site // grid.cores, grid.ny)
            for dx, dy in keys:

                @pl.when(behind == dy)
                def _():
                    pltpu.make_async_copy(pieces[dx, dy], out_ref.at[k, dx], in_sems.at[k, dx]).start()

        for k in range(len(sites)):
            for dx in range(grid.nx):
                pltpu.make_async_copy(refs[0], out_ref.at[k, dx], in_sems.at[k, dx]).wait()


def collect(grid, sites, pieces, token=()):
    nx = grid.nx
    keys = tuple(pieces)
    tall, width = pieces[0, 0].shape
    if grid.kernels:
        hbm = pl.BlockSpec(memory_space=pl.ANY)
        shape = (len(sites), nx, tall, width)
        operands = list(pieces.values()) + list(token)
        return pl.pallas_call(
            functools.partial(collect_kernel, grid, tuple(sites), keys),
            out_shape=jax.ShapeDtypeStruct(shape, jnp.float32),
            in_specs=[hbm] * len(operands),
            out_specs=pl.BlockSpec(memory_space=pltpu.VMEM),
            scratch_shapes=[
                pltpu.SemaphoreType.DMA(shape[:2]),
            ],
            compiler_params=pltpu.CompilerParams(vmem_limit_bytes=32 * 1024 * 1024),
            cost_estimate=pl.CostEstimate(flops=0, bytes_accessed=8 * len(sites) * nx * tall * width, transcendentals=0),
        )(*operands)
    mats = []
    for site in sites:
        behind = (grid.here()[2] - site // grid.cores) % grid.ny
        for dx in range(nx):
            value = pieces[dx, 0]
            for dy in range(1, grid.ny):
                value = jnp.where(behind == dy, pieces[dx, dy], value)
            mats.append(value)
    return jnp.stack(mats).reshape(len(sites), nx, tall, width)


def site_kernel(grid, site, last, tokens, *refs):
    nx, ny, nz, rows, strip, share = grid.nx, grid.ny, grid.nz, grid.rows, grid.strip, grid.share
    mats, refs = refs[: grid.cores], refs[grid.cores :]
    states, refs = refs[:nz], refs[nz + tokens :]
    outs = refs[: nx * ny]
    mat_ref, state_ref, high_ref, low_ref, sems, state_sems = refs[nx * ny :]
    z, _, y, core = grid.here()
    place = site // grid.cores
    inward = []
    for n, source in enumerate(grid.gathered_from(z)):
        at = pl.ds(pl.multiple_of(source * strip, strip), strip)
        inward.append(pltpu.make_async_copy(states[n], state_ref.at[at], state_sems.at[n]))
        inward[-1].start()

    for role, ref in enumerate(mats):

        @pl.when(core == role)
        def _():
            for dx in range(nx):
                pltpu.make_async_copy(ref.at[place, dx], mat_ref.at[dx], sems.at[dx]).start()

    for copy in inward:
        copy.wait()
    high_ref[...], low_ref[...] = halves(state_ref[...])
    for ex in range(nx):
        dx = (nx - ex) % nx
        pltpu.make_async_copy(mats[0].at[place, dx], mat_ref.at[dx], sems.at[dx]).wait()
        if ex == 0:
            clicks = mat_ref[0, 2 * rows : 2 * rows + CLICK_ROWS, :]
            row = lax.broadcasted_iota(jnp.int32, clicks.shape, 0)
            clicks = jnp.sum(jnp.where(row == core, clicks, 0.0), axis=0, keepdims=True)
        for ey in range(ny):
            to = lax.rem(y + ey, ny)
            out_ref = outs[ex * ny + ey]
            if last:
                columns = pl.ds(pl.multiple_of(to * share, share), share)
                b = (high_ref[:, columns], low_ref[:, columns])
                picked = jnp.zeros((1, share), jnp.float32)
                for yy in range(ny):
                    picked = jnp.where(to == yy, clicks[:, yy * share : (yy + 1) * share], picked)
                both = [dot3(halves(mat_ref[dx, o * rows : (o + 1) * rows, :]), b) for o in range(2)]
                out_ref[...] = jnp.where(picked == 1, both[1], both[0])
            else:
                at = pl.multiple_of(to * strip, strip)
                b = (high_ref[...], low_ref[...])
                both = [dot3(halves(mat_ref[dx, pl.ds(o * rows + at, strip), :]), b) for o in range(2)]
                out_ref[...] = jnp.where(clicks == 1, both[1], both[0])


def site_product(grid, site, clicks, mats, states, token=()):
    nx, ny, nz, rows, width, cols = grid.nx, grid.ny, grid.nz, grid.rows, grid.width, grid.cols
    last = site == grid.sites - 1
    shape = (rows, grid.share) if last else (grid.strip, cols)
    if grid.kernels:
        vmem, hbm = pl.BlockSpec(memory_space=pltpu.VMEM), pl.BlockSpec(memory_space=pl.ANY)
        tall = grid.rows * 2 + CLICK_ROWS
        flops = 2 * 3 * 2 * nx * rows * width * cols
        moved = 4 * (nx * tall * width + width * cols + nx * rows * cols)
        return pl.pallas_call(
            functools.partial(site_kernel, grid, site, last, len(token)),
            out_shape=[jax.ShapeDtypeStruct(shape, jnp.float32)] * (nx * ny),
            in_specs=[hbm] * (len(mats) + nz + len(token)),
            out_specs=[vmem] * (nx * ny),
            scratch_shapes=[
                pltpu.VMEM((nx, tall, width), jnp.float32),
                pltpu.VMEM((width, cols), jnp.float32),
                pltpu.VMEM((width, cols), jnp.bfloat16),
                pltpu.VMEM((width, cols), jnp.bfloat16),
                pltpu.SemaphoreType.DMA((nx,)),
                pltpu.SemaphoreType.DMA((nz,)),
            ],
            compiler_params=pltpu.CompilerParams(vmem_limit_bytes=32 * 1024 * 1024),
            cost_estimate=pl.CostEstimate(flops=flops, bytes_accessed=moved, transcendentals=0),
        )(*mats, *states, *token)
    z, _, y, core = grid.here()
    whole = jnp.zeros((width, cols), jnp.float32)
    for value, source in zip(states, grid.gathered_from(z)):
        whole = lax.dynamic_update_slice_in_dim(whole, value, source * grid.strip, 0)
    outs = []
    for ex in range(nx):
        dx = (nx - ex) % nx
        mat = 0
        for role, value in enumerate(mats):
            mat = jnp.where(core == role, value[site // grid.cores, dx], mat)
        both = jnp.dot(mat, whole, precision=lax.Precision.HIGH, preferred_element_type=jnp.float32)
        picked = jnp.where(clicks == 1, both[rows:], both[:rows])
        for ey in range(ny):
            axis = 1 if last else 0
            outs.append(lax.dynamic_slice_in_dim(picked, ((y + ey) % ny) * shape[axis], shape[axis], axis))
    return outs


def local(left_start, site_mats, clicks):
    sites, bonds = lax.axis_size("site"), lax.axis_size("bond")
    grid = Grid(sites, bonds, site_mats.shape[2], left_start.shape[1])
    nx, ny, nz, cores = grid.nx, grid.ny, grid.nz, grid.cores
    _, _, y, core = grid.here()
    pieces, state = pack(grid, clicks, site_mats[0], left_start)
    shifts = [(dx, dy) for dx in range(nx) for dy in range(ny)]

    own_clicks = {}
    if not grid.kernels:
        for dy in range(ny):
            for dcore in range(cores):
                own_clicks[dy, dcore] = grid.send(clicks, dy=dy, dcore=dcore) if dy or dcore else clicks

    def clicks_of(site):
        value = clicks
        for (dy, dcore), got in own_clicks.items():
            hit = ((y - site // cores) % ny == dy) & ((core - site % cores) % cores == dcore)
            value = jnp.where(hit, got, value)
        return own_samples(grid, value)

    def spread(which, pieces):
        got, own = {}, pieces[0]
        for dx, dy in shifts[:0:-1]:
            if which and not (dx and dy) and (nx - 1, ny - 1) in got:
                got[nx - 1, ny - 1], pieces = lax.optimization_barrier((got[nx - 1, ny - 1], pieces))
            got[dx, dy] = grid.send(pieces[dx * ny + dy], dx=dx, dy=dy, cores=[which])
        return {(0, 0): own, **got}

    def across(mine, which):
        others = [grid.send(mine, dcore=d, cores=[which]) for d in range(1, cores)]
        return [([mine] + others)[(role - which) % cores] for role in range(cores)]

    mats = []
    for site in range(sites):
        gathered = grid.gather(state, relay=RELAY[min(site, 3)])
        token = []
        if site == 0:
            got = spread(0, pieces)
            mats.append(across(collect(grid, range(0, sites, cores), got, gathered), 0))
            for which in range(1, cores):
                gathered, after, later = lax.optimization_barrier((gathered, list(got.values())[1:], pieces))
                got = spread(which, later)
                token += [got[0, 1]] + after
        outs = site_product(grid, site, clicks_of(site), mats[site % cores], gathered, token)
        if site == 0 and cores > 1:
            mats.append(across(collect(grid, range(1, sites, cores), got, outs[:1]), 1))
        state = outs[0]
        for ex, ey in shifts[:0:-1]:
            state = state + grid.send(outs[ex * ny + ey], dx=ex, dy=ey)
    return state


def solution(mesh):
    return jax.shard_map(
        local,
        mesh=mesh,
        in_specs=(P("bond", None), P("site", None, "bond", None), P("site", None)),
        out_specs=P("bond", "site"),
        check_vma=False,
    )
```
